256 devices in a mesh: dom: 64 (over y, x_hi, z), rep: 4 (over x_lo, core).
Axes of the slice: x: 4 (x_hi: 2, x_lo: 2; x = x_hi * 2 + x_lo), y: 4, z: 8, core: 2. Of those that a mesh axis runs over, the one named last changes fastest.
Arguments:
- entities: float32 [32768, 384], P('dom'), may hold values from -1.8 to 1.8
- entity_state: float32 [32768], P('dom'), may hold values from 0.01 to 1
- relations: float32 [7424, 384], P(('dom', 'rep')), may hold values from -1.8 to 1.8
- relation_state: float32 [7424], P(('dom', 'rep')), may hold values from 0.01 to 1
- head_ids: int32 [512000], P(('dom', 'rep')), may hold values from 0 to 511
- relation_ids: int32 [512000], P(('dom', 'rep')), may hold values from 0 to 7423
- tail_ids: int32 [512000], P(('dom', 'rep')), may hold values from 0 to 511
- head_negatives: int32 [512, 1000], P(('dom', 'rep')), may hold values from 0 to 511
- tail_negatives: int32 [512, 1000], P(('dom', 'rep')), may hold values from 0 to 511
- bucket_sizes: int32 [64], P('dom'), may hold values from 1000 to 8000, as said below
- plan: int32 [64], replicated, may hold values from 0 to 63, as said below
Outputs:
- new_entities: float32 [32768, 384], P('dom')
- new_entity_state: float32 [32768], P('dom')
- new_relations: float32 [7424, 384], P(('dom', 'rep'))
- new_relation_state: float32 [7424], P(('dom', 'rep'))
The draws below stay inside these ranges and needn't reach their ends.
Inputs may be any that keep to these rules, and one draw needn't show every extreme that they name: `bucket_sizes`: the largest bucket is full: some bucket has 8000 live slots in every draw; each has at least an eighth of that. plan[p] = p XOR m for one m, the same for all p, with 1 <= m < 64; so plan is its own inverse and has no fixed point.
All inputs are finite; a program needn't handle non-finite values.
Results may differ from the reference program's by a relative error of at most 0.0034.
Values may be sent and summed in bfloat16 or wider, within the bound.
A program may use at most 128 MiB of HBM per device.

```python
import math
import jax
import jax.numpy as jnp
from jax import lax

K = 384
R = 7424
GROUP = 1000
NEG = 1000
CH_DEV = 2
E_DEV = 512
B_DEV = 2000
ENTITIES = 32768
EDGES = 512000
BLOCKS = 512
N_DOM = 64
N_REP = 4


def draw_bucket_sizes(key, part):
    key = jax.random.fold_in(key, 11)
    first_key, second_key = jax.random.split(key)
    filled = B_DEV * N_REP
    counts = jax.random.randint(first_key, (N_DOM,), filled // 8, filled + 1)
    chosen = jax.random.randint(second_key, (), 0, N_DOM)
    return jnp.where(jnp.arange(N_DOM) == chosen, filled, counts).astype(jnp.int32)


def draw_plan(key, part):
    key = jax.random.fold_in(key, 13)
    offset = jax.random.randint(key, (), 1, N_DOM)
    return jnp.bitwise_xor(jnp.arange(N_DOM, dtype=jnp.int32), offset.astype(jnp.int32)).astype(jnp.int32)


def set_ends(array, rng, smallest, high):
    spot = [jax.random.randint(jax.random.fold_in(rng, axis), (), 0, length) for axis, length in enumerate(array.shape)]
    longest = array.shape.index(max(array.shape))
    beside = spot[:longest] + [(spot[longest] + 1) % array.shape[longest]] + spot[longest + 1:]
    return array.at[tuple(spot)].set(smallest).at[tuple(beside)].set(high)


def level_of(rng, extent, pieces, low, top_value):
    loudness, own = 1.0, jax.random.fold_in(rng, 6)
    for axis_at, blocks in pieces:
        heights = jnp.exp(jax.random.uniform(jax.random.fold_in(own, axis_at), (blocks,), jnp.float32, low / len(pieces), top_value / len(pieces)))
        loudness = loudness * jnp.repeat(heights, extent[axis_at] // blocks).reshape([-1 if axis == axis_at else 1 for axis in range(len(extent))])
    return loudness


def bell_draw(key, dims, scale, most, shards=(), kind=jnp.bfloat16):
    array = scale * jax.random.normal(key, dims, jnp.float32)
    if shards:
        array = array * level_of(key, dims, shards, -0.22, 0.18)
    return jnp.clip(array, -most, most).astype(kind)


def setup_inputs(seed: int = 0) -> dict:
    splits = jax.random.split(jax.random.key(seed), 12)
    entities = bell_draw(splits[0], (ENTITIES, K), 0.3, 1.8, ((0, 64),), jnp.float32)
    entity_state = jnp.clip(jnp.exp(math.log(1.0) - 4.6051702 * jax.random.uniform(splits[1], (ENTITIES,), jnp.float32) ** level_of(splits[1], (ENTITIES,), ((0, 64),), -0.2, 0.2)), 0.01, 1.0)
    relations = bell_draw(splits[2], (R, K), 0.3, 1.8, ((0, 256),), jnp.float32)
    relation_state = jnp.clip(jnp.exp(math.log(1.0) - 4.6051702 * jax.random.uniform(splits[3], (R,), jnp.float32) ** level_of(splits[3], (R,), ((0, 256),), -0.2, 0.2)), 0.01, 1.0)
    head_ids = set_ends(jax.random.randint(splits[4], (EDGES,), 0, E_DEV), jax.random.fold_in(splits[4], 1), 0, E_DEV - 1).astype(jnp.int32)
    relation_ids = set_ends(jax.random.randint(splits[5], (EDGES,), 0, R), jax.random.fold_in(splits[5], 1), 0, R - 1).astype(jnp.int32)
    tail_ids = set_ends(jax.random.randint(splits[6], (EDGES,), 0, E_DEV), jax.random.fold_in(splits[6], 1), 0, E_DEV - 1).astype(jnp.int32)
    head_negatives = set_ends(jax.random.randint(splits[7], (BLOCKS, NEG), 0, E_DEV), jax.random.fold_in(splits[7], 1), 0, E_DEV - 1).astype(jnp.int32)
    tail_negatives = set_ends(jax.random.randint(splits[8], (BLOCKS, NEG), 0, E_DEV), jax.random.fold_in(splits[8], 1), 0, E_DEV - 1).astype(jnp.int32)
    bucket_sizes = draw_bucket_sizes(jax.random.fold_in(splits[11], 71), 0)
    plan = draw_plan(jax.random.fold_in(splits[11], 71), 0)
    return {"entities": entities, "entity_state": entity_state, "relations": relations, "relation_state": relation_state, "head_ids": head_ids, "relation_ids": relation_ids, "tail_ids": tail_ids, "head_negatives": head_negatives, "tail_negatives": tail_negatives, "bucket_sizes": bucket_sizes, "plan": plan}


LEARN = 0.1

def split_halves(rows):
    half = rows.shape[1] // 2
    return (rows[:, :half], rows[:, half:])

def edge_gradients(head_rows, relation_rows, tail_rows, head_negs, tail_negs, active):
    head_full = head_rows.astype(jnp.float32)
    tail_full = tail_rows.astype(jnp.float32)
    head_real, head_imag = split_halves(head_full)
    rel_real, rel_imag = split_halves(relation_rows.astype(jnp.float32))
    tail_real, tail_imag = split_halves(tail_full)
    query = jnp.concatenate([head_real * rel_real - head_imag * rel_imag, head_real * rel_imag + head_imag * rel_real], axis=1)
    probe = jnp.concatenate([rel_real * tail_real + rel_imag * tail_imag, rel_real * tail_imag - rel_imag * tail_real], axis=1)
    positive = lax.optimization_barrier(jnp.sum(query * tail_full, axis=1))
    query_low = query.astype(jnp.bfloat16)
    probe_low = probe.astype(jnp.bfloat16)
    inner = (((1,), (1,)), ((), ()))
    outer = (((0,), (0,)), ((), ()))
    tail_scores = lax.dot_general(query_low, tail_negs, inner, preferred_element_type=jnp.float32)
    head_scores = lax.dot_general(probe_low, head_negs, inner, preferred_element_type=jnp.float32)
    samples = tail_negs.shape[0]
    pos_weight = -active * jax.nn.sigmoid(-positive)
    scaling = (active / samples)[:, None]
    tail_weight = (jax.nn.sigmoid(tail_scores) * scaling).astype(jnp.bfloat16)
    head_weight = (jax.nn.sigmoid(head_scores) * scaling).astype(jnp.bfloat16)
    query_grad = pos_weight[:, None] * tail_full + jnp.dot(tail_weight, tail_negs, preferred_element_type=jnp.float32)
    probe_grad = jnp.dot(head_weight, head_negs, preferred_element_type=jnp.float32)
    tail_neg_grad = lax.dot_general(tail_weight, query_low, outer, preferred_element_type=jnp.float32)
    head_neg_grad = lax.dot_general(head_weight, probe_low, outer, preferred_element_type=jnp.float32)
    qg_real, qg_imag = split_halves(query_grad)
    pg_real, pg_imag = split_halves(probe_grad)
    head_grad = jnp.concatenate([qg_real * rel_real + qg_imag * rel_imag, qg_imag * rel_real - qg_real * rel_imag], axis=1)
    tail_grad = jnp.concatenate([pg_real * rel_real - pg_imag * rel_imag, pg_real * rel_imag + pg_imag * rel_real], axis=1) + pos_weight[:, None] * query
    relation_grad = jnp.concatenate([qg_real * head_real + qg_imag * head_imag + pg_real * tail_real + pg_imag * tail_imag, qg_imag * head_real - qg_real * head_imag + pg_real * tail_imag - pg_imag * tail_real], axis=1)
    return (head_grad, tail_grad, relation_grad, head_neg_grad, tail_neg_grad)

def adagrad(param, state, grad):
    new_state = state + lax.optimization_barrier(jnp.mean(grad * grad, axis=1))
    return (param - LEARN * grad / jnp.sqrt(new_state)[:, None], new_state)

def reference(entities, entity_state, relations, relation_state, head_ids, relation_ids, tail_ids, head_negatives, tail_negatives, bucket_sizes, plan):
    entity_low = entities.astype(jnp.bfloat16)
    relation_low = relations.astype(jnp.bfloat16)
    width = entities.shape[1]

    def one_bucket(bucket, carry):
        entity_sum, relation_sum = carry
        bucket = jnp.asarray(bucket).astype(jnp.int32)
        partner = plan[bucket].astype(jnp.int32)
        own_rows = lax.dynamic_slice_in_dim(entity_low, (bucket * E_DEV).astype(jnp.int32), E_DEV, 0)
        partner_rows = lax.dynamic_slice_in_dim(entity_low, (partner * E_DEV).astype(jnp.int32), E_DEV, 0)
        own_grad = jnp.zeros((E_DEV, width), jnp.float32)
        partner_grad = jnp.zeros((E_DEV, width), jnp.float32)
        for replica in range(N_REP):
            for block in range(CH_DEV):
                first = ((bucket * N_REP + replica) * B_DEV + block * GROUP).astype(jnp.int32)
                heads_here = lax.dynamic_slice_in_dim(head_ids, first, GROUP, 0).astype(jnp.int32)
                rels_here = lax.dynamic_slice_in_dim(relation_ids, first, GROUP, 0).astype(jnp.int32)
                tails_here = lax.dynamic_slice_in_dim(tail_ids, first, GROUP, 0).astype(jnp.int32)
                slots = replica * B_DEV + block * GROUP + jnp.arange(GROUP, dtype=jnp.int32)
                active = (slots < bucket_sizes[bucket]).astype(jnp.float32)
                row_index = ((bucket * N_REP + replica) * CH_DEV + block).astype(jnp.int32)
                negs_head = lax.dynamic_index_in_dim(head_negatives, row_index, 0, keepdims=False).astype(jnp.int32)
                negs_tail = lax.dynamic_index_in_dim(tail_negatives, row_index, 0, keepdims=False).astype(jnp.int32)
                grads = edge_gradients(jnp.take(own_rows, heads_here, axis=0), jnp.take(relation_low, rels_here, axis=0), jnp.take(partner_rows, tails_here, axis=0), jnp.take(own_rows, negs_head, axis=0), jnp.take(partner_rows, negs_tail, axis=0), active)
                head_grad, tail_grad, relation_grad, head_neg_grad, tail_neg_grad = grads
                own_grad = own_grad + jax.ops.segment_sum(head_grad, heads_here, num_segments=E_DEV) + jax.ops.segment_sum(head_neg_grad, negs_head, num_segments=E_DEV)
                partner_grad = partner_grad + jax.ops.segment_sum(tail_grad, tails_here, num_segments=E_DEV) + jax.ops.segment_sum(tail_neg_grad, negs_tail, num_segments=E_DEV)
                relation_sum = relation_sum + jax.ops.segment_sum(relation_grad, rels_here, num_segments=R)
        own_first = (bucket * E_DEV).astype(jnp.int32)
        own_total = lax.dynamic_slice_in_dim(entity_sum, own_first, E_DEV, 0) + own_grad
        entity_sum = lax.dynamic_update_slice_in_dim(entity_sum, own_total, own_first, 0)
        partner_first = (partner * E_DEV).astype(jnp.int32)
        partner_total = lax.dynamic_slice_in_dim(entity_sum, partner_first, E_DEV, 0) + partner_grad
        entity_sum = lax.dynamic_update_slice_in_dim(entity_sum, partner_total, partner_first, 0)
        return (entity_sum, relation_sum)
    start_carry = (jnp.zeros((E_DEV * N_DOM, width), jnp.float32), jnp.zeros((R, width), jnp.float32))
    entity_sum, relation_sum = lax.fori_loop(0, N_DOM, one_bucket, start_carry)
    new_entities, new_entity_state = adagrad(entities, entity_state, entity_sum)
    new_relations, new_relation_state = adagrad(relations, relation_state, relation_sum)
    return (new_entities, new_entity_state, new_relations, new_relation_state)
```

```python
import functools

import jax
import jax.numpy as jnp
from jax import lax
from jax.experimental import pallas as pl
from jax.experimental.pallas import tpu as pltpu
from jax.sharding import PartitionSpec as P

LEARN = 0.1
NX, NY, NZ, NC = 4, 4, 8, 2
SLOT = 32
LANES = 128
PARTS = 3
SIZES = {"x": NX, "y": NY, "z": NZ}
ORDERS = (("z", "y", "x"), ("x", "z", "y"), ("y", "x", "z"))
MESH = pl.DeviceIdType.MESH
VMEM_LIMIT = 56 * 1024 * 1024


def here():
    dom = lax.axis_index("dom")
    rep = lax.axis_index("rep")
    pos = {
        "y": dom // (2 * NZ),
        "x": lax.rem(dom // NZ, 2) * 2 + rep // 2,
        "z": lax.rem(dom, NZ),
    }
    return pos, lax.rem(rep, 2)


def device(pos, core):
    dom = pos["y"] * (2 * NZ) + (pos["x"] // 2) * NZ + pos["z"]
    rep = lax.rem(pos["x"], 2) * 2 + core
    return (dom, rep)


def moved(pos, axis, offset):
    there = dict(pos)
    there[axis] = lax.rem(pos[axis] + offset + SIZES[axis], SIZES[axis])
    return there


def greet(devices):
    barrier = pltpu.get_barrier_semaphore()
    for target in devices:
        pl.semaphore_signal(barrier, inc=1, device_id=target, device_id_type=MESH)
    pl.semaphore_wait(barrier, len(devices))


def all_peers(pos, core):
    peers = [device(pos, 1 - core)]
    for axis, count in SIZES.items():
        peers += [device(moved(pos, axis, step), core) for step in range(1, count)]
    return peers


def region(pos, free):
    return tuple(slice(None) if axis in free else pos[axis] for axis in ("y", "x", "z"))


class Sems:
    def __init__(self, send, recv):
        self.send, self.recv, self.used = send, recv, 0

    def copy(self, source, target, device_id):
        index = self.used
        self.used += 1
        return pltpu.make_async_remote_copy(
            src_ref=source,
            dst_ref=target,
            send_sem=self.send.at[index],
            recv_sem=self.recv.at[index],
            device_id=device_id,
            device_id_type=MESH,
        )


GATHER_COPIES = 80


def gather_kernel(rel_ref, piece_ref, table_ref, partner_ref, send, recv, local_sem):
    pos, core = here()
    sems = Sems(send, recv)
    pending = []

    def put(source, device_id):
        copy = sems.copy(source, source, device_id)
        copy.start()
        pending.append(copy)
        return copy

    mine = region(pos, ())
    for part in range(PARTS):
        table_ref[(part, core) + mine] = rel_ref[part]
    x_low = lax.rem(pos["x"], 2)
    partner_ref[x_low, core] = piece_ref[...]
    greet(all_peers(pos, core))

    def block(part, which, free):
        return table_ref.at[(part, which) + region(pos, free)]

    def block_at(part, where, free):
        return table_ref.at[(part, core) + region(where, free)]

    sibling = device(pos, 1 - core)
    side = dict(pos)
    side["x"] = pos["x"] + 1 - 2 * x_low

    stage = []
    for part in range(PARTS):
        axis = ORDERS[part][0]
        stage.append(
            [
                put(block(part, core, ()), device(moved(pos, axis, step), core))
                for step in range(1, SIZES[axis])
            ]
        )
    piece_side = put(partner_ref.at[x_low, core], device(side, core))
    second = []
    for part in range(PARTS):
        for copy in stage[part]:
            copy.wait_recv()
        free = ORDERS[part][:1]
        axis = ORDERS[part][1]
        second.append(
            [
                put(block(part, core, free), device(moved(pos, axis, step), core))
                for step in range(1, SIZES[axis])
            ]
        )
    piece_side.wait_recv()
    piece_core = put(partner_ref.at[:, core], sibling)
    third = []
    for part in range(PARTS):
        for copy in second[part]:
            copy.wait_recv()
        free = ORDERS[part][:2]
        axis = ORDERS[part][2]
        if axis != "z":
            third.append(
                [
                    put(block(part, core, free), device(moved(pos, axis, step), core))
                    for step in range(1, SIZES[axis])
                ]
            )
    last = PARTS - 1
    free = ORDERS[last][:2]
    right = device(moved(pos, "z", 1), core)
    left = device(moved(pos, "z", -1), core)
    to_right = put(block(last, core, free), right)
    to_left = put(block(last, core, free), left)
    across = [put(block(part, core, ORDERS[part][:2]), sibling) for part in range(PARTS)]
    for step in range(1, 4):
        to_right.wait_recv()
        from_left = block_at(last, moved(pos, "z", -step), free)
        to_right = put(from_left, right)
        across.append(put(from_left, sibling))
        to_left.wait_recv()
        from_right = block_at(last, moved(pos, "z", step), free)
        if step < 3:
            to_left = put(from_right, left)
        across.append(put(from_right, sibling))
    for part in range(2):
        axis = ORDERS[part][2]
        for step in range(1, SIZES[axis]):
            third[part][step - 1].wait_recv()
            arrived = block_at(part, moved(pos, axis, -step), ORDERS[part][:2])
            across.append(put(arrived, sibling))
    to_right.wait_recv()
    across.append(put(block_at(last, moved(pos, "z", -4), free), sibling))
    piece_core.wait_recv()
    for copy in across:
        copy.wait_recv()
    for copy in pending:
        copy.wait_send()


def gather_tables(rel, piece):
    count = GATHER_COPIES
    vmem = pl.BlockSpec(memory_space=pltpu.VMEM)
    return pl.pallas_call(
        gather_kernel,
        out_shape=(
            jax.ShapeDtypeStruct((PARTS, NC, NY, NX, NZ, SLOT, LANES), jnp.bfloat16),
            jax.ShapeDtypeStruct((2, NC) + piece.shape, jnp.bfloat16),
        ),
        in_specs=[vmem] * 2,
        out_specs=(vmem, vmem),
        scratch_shapes=[
            pltpu.SemaphoreType.DMA((count,)),
            pltpu.SemaphoreType.DMA((count,)),
            pltpu.SemaphoreType.DMA,
        ],
        compiler_params=pltpu.CompilerParams(
            collective_id=0, has_side_effects=True, vmem_limit_bytes=VMEM_LIMIT
        ),
    )(rel, piece)


ROWS = NC * NY * NX * NZ * SLOT
TILE = 512
CHUNK = 1024
INNER = (((1,), (1,)), ((), ()))
FIRST = (((0,), (0,)), ((), ()))


def dot(a, b, dims=(((1,), (0,)), ((), ()))):
    return lax.dot_general(a, b, dims, preferred_element_type=jnp.float32)


def one_hot(ids, base, count):
    rows = lax.broadcasted_iota(jnp.int32, (count, ids.shape[1]), 0)
    return jnp.where(rows == ids - base, 1.0, 0.0).astype(jnp.bfloat16)


def compute_kernel(
    samples,
    ids_ref,
    act_ref,
    negs_ref,
    own_ref,
    par_ref,
    table_ref,
    head_ref,
    tail_ref,
    rel_out_ref,
    w_ref,
    rg_ref,
    own_t,
    par_t,
    count_ref,
    head_acc,
    tail_acc,
):
    ent = own_ref.shape[0]
    half = own_ref.shape[1] // 2
    lanes = ids_ref.shape[1]
    own_t[...] = own_ref[...].astype(jnp.float32).T.astype(jnp.bfloat16)
    par_t[...] = par_ref[...].astype(jnp.float32).T.astype(jnp.bfloat16)
    ones = jnp.ones((negs_ref.shape[1], LANES), jnp.bfloat16)
    for row in range(4):
        count_ref[row] = dot(one_hot(negs_ref[row : row + 1, :], 0, ent), ones)

    w_ref[...] = jnp.zeros_like(w_ref)

    @pl.loop(0, ROWS // CHUNK)
    def _(index):
        base = pl.multiple_of(index * CHUNK, CHUNK)
        rows = jnp.concatenate(
            [table_ref[part, pl.ds(base, CHUNK), :] for part in range(PARTS)], axis=1
        )
        hot = one_hot(ids_ref[1:2, :], base, CHUNK)
        w_ref[...] += dot(rows, hot, FIRST)

    head_acc[...] = jnp.zeros_like(head_acc)
    tail_acc[...] = jnp.zeros_like(tail_acc)

    @pl.loop(0, lanes // TILE)
    def _(tile):
        base = pl.multiple_of(tile * TILE, TILE)
        cols = pl.ds(base, TILE)
        block = tile // (lanes // TILE // 2)
        hot_h = one_hot(ids_ref[0:1, cols], 0, ent)
        hot_t = one_hot(ids_ref[2:3, cols], 0, ent)
        act = act_ref[0:1, cols]
        h = dot(own_t[...], hot_h)
        t = dot(par_t[...], hot_t)
        w = w_ref[:, cols]
        ha, hb, ta, tb, wa, wb = h[:half], h[half:], t[:half], t[half:], w[:half], w[half:]
        query = jnp.concatenate([ha * wa - hb * wb, ha * wb + hb * wa], axis=0)
        probe = jnp.concatenate([wa * ta + wb * tb, wa * tb - wb * ta], axis=0)
        positive = jnp.sum(query * t, axis=0, keepdims=True)
        query_low = query.astype(jnp.bfloat16)
        probe_low = probe.astype(jnp.bfloat16)
        pos_weight = -act * jax.nn.sigmoid(-positive)
        scaling = act / samples

        def weights(scores, row):
            count = jnp.concatenate([count_ref[row]] * (TILE // LANES), axis=1)
            return (jax.nn.sigmoid(scores) * scaling * count).astype(jnp.bfloat16)

        tail_w = weights(dot(par_ref[...], query_low), 2 + block)
        head_w = weights(dot(own_ref[...], probe_low), block)
        qg = pos_weight * t + dot(par_t[...], tail_w)
        pg = dot(own_t[...], head_w)
        qa, qb, pa, pb = qg[:half], qg[half:], pg[:half], pg[half:]
        head_grad = jnp.concatenate([qa * wa + qb * wb, qb * wa - qa * wb], axis=0)
        tail_grad = (
            jnp.concatenate([pa * wa - pb * wb, pa * wb + pb * wa], axis=0) + pos_weight * query
        )
        rel_grad = jnp.concatenate(
            [qa * ha + qb * hb + pa * ta + pb * tb, qb * ha - qa * hb + pa * tb - pb * ta], axis=0
        )
        rg_ref[:, cols] = rel_grad.astype(jnp.bfloat16)
        head_acc[...] += dot(head_w, probe_low, INNER) + dot(
            hot_h, head_grad.astype(jnp.bfloat16), INNER
        )
        tail_acc[...] += dot(tail_w, query_low, INNER) + dot(
            hot_t, tail_grad.astype(jnp.bfloat16), INNER
        )

    head_ref[...] = head_acc[...].astype(jnp.bfloat16)
    tail_ref[...] = tail_acc[...].astype(jnp.bfloat16)

    @pl.loop(0, ROWS // CHUNK)
    def _(index):
        base = pl.multiple_of(index * CHUNK, CHUNK)
        hot = one_hot(ids_ref[1:2, :], base, CHUNK)
        summed = dot(hot, rg_ref[...], INNER).astype(jnp.bfloat16)
        for part in range(PARTS):
            rel_out_ref[part, pl.ds(base, CHUNK), :] = summed[
                :, part * LANES : (part + 1) * LANES
            ]


def compute(ids, act, negs, own, par, table, samples):
    vmem = pl.BlockSpec(memory_space=pltpu.VMEM)
    ent, width = own.shape
    lanes = ids.shape[1]
    return pl.pallas_call(
        functools.partial(compute_kernel, samples),
        out_shape=(
            jax.ShapeDtypeStruct((ent, width), jnp.bfloat16),
            jax.ShapeDtypeStruct((ent, width), jnp.bfloat16),
            jax.ShapeDtypeStruct((PARTS, ROWS, LANES), jnp.bfloat16),
        ),
        in_specs=[vmem] * 6,
        out_specs=(vmem,) * 3,
        scratch_shapes=[
            pltpu.VMEM((width, lanes), jnp.float32),
            pltpu.VMEM((width, lanes), jnp.bfloat16),
            pltpu.VMEM((width, ent), jnp.bfloat16),
            pltpu.VMEM((width, ent), jnp.bfloat16),
            pltpu.VMEM((4, ent, LANES), jnp.float32),
            pltpu.VMEM((ent, width), jnp.float32),
            pltpu.VMEM((ent, width), jnp.float32),
        ],
        compiler_params=pltpu.CompilerParams(vmem_limit_bytes=VMEM_LIMIT),
    )(ids, act, negs, own, par, table)


SCATTER_COPIES = 80


def scatter_kernel(
    rel_ref,
    ent_ref,
    rel_sum_ref,
    ent_sum_ref,
    from_core,
    total,
    in_x,
    in_y,
    in_z,
    out_z,
    two_0,
    in_0,
    two_1,
    in_1,
    two_2,
    in_2,
    last_0,
    last_1,
    last_2,
    end_0,
    end_1,
    end_2,
    ent_core,
    ent_half,
    ent_side,
    send,
    recv,
):
    f32, bf16 = jnp.float32, jnp.bfloat16
    pos, core = here()
    sems = Sems(send, recv)
    pending = []

    def put(source, target, device_id):
        copy = sems.copy(source, target, device_id)
        copy.start()
        pending.append(copy)
        return copy

    x_low = lax.rem(pos["x"], 2)
    sibling = device(pos, 1 - core)
    side = dict(pos)
    side["x"] = pos["x"] + 1 - 2 * x_low
    greet(all_peers(pos, core))

    ent_copy = put(ent_ref.at[:, :, 1 - core], ent_core, sibling)
    order = [2, 0, 1]
    core_copies = {
        part: put(rel_ref.at[part, 1 - core], from_core.at[part], sibling) for part in order
    }
    ent_copy.wait_recv()
    ent_half[...] = (
        ent_ref[:, :, pl.ds(core, 1)][:, :, 0].astype(f32) + ent_core[...].astype(f32)
    ).astype(bf16)
    side_copy = put(ent_half.at[:, 1 - x_low], ent_side, device(side, core))

    def add_cores(part):
        core_copies[part].wait_recv()

        @pl.loop(0, NY)
        def _(y):
            total[part, y] = (
                rel_ref[part, core, y].astype(f32) + from_core[part, y].astype(f32)
            ).astype(bf16)

    add_cores(2)
    right = device(moved(pos, "z", 1), core)
    left = device(moved(pos, "z", -1), core)

    def z_term(offset):
        return total[2, :, :, moved(pos, "z", offset)["z"]]

    out_z[0] = z_term(4)
    to_right = put(out_z.at[0], in_z.at[0], right)
    out_z[4] = z_term(-3)
    to_left = put(out_z.at[4], in_z.at[4], left)

    add_cores(0)
    first_x = []
    for step in range(1, NX):
        there = moved(pos, "x", step)
        first_x.append(put(total.at[0, :, there["x"]], in_x.at[step - 1], device(there, core)))
    add_cores(1)
    first_y = []
    for step in range(1, NY):
        there = moved(pos, "y", step)
        first_y.append(put(total.at[1, there["y"]], in_y.at[step - 1], device(there, core)))

    for step in range(1, 4):
        to_right.wait_recv()
        out_z[step] = (
            in_z[step - 1].astype(f32) + z_term(4 - step).astype(f32)
        ).astype(bf16)
        to_right = put(out_z.at[step], in_z.at[step], right)
        to_left.wait_recv()
        if step < 3:
            out_z[4 + step] = (
                in_z[3 + step].astype(f32) + z_term(step - 3).astype(f32)
            ).astype(bf16)
            to_left = put(out_z.at[4 + step], in_z.at[4 + step], left)
    to_right.wait_recv()
    two_2[...] = (
        z_term(0).astype(f32) + in_z[3].astype(f32) + in_z[6].astype(f32)
    ).astype(bf16)
    second_2 = []
    for step in range(1, NX):
        there = moved(pos, "x", step)
        second_2.append(put(two_2.at[:, there["x"]], in_2.at[step - 1], device(there, core)))

    for copy in first_x:
        copy.wait_recv()
    value = total[0, :, pos["x"]].astype(f32)
    for step in range(NX - 1):
        value += in_x[step].astype(f32)
    two_0[...] = value.astype(bf16)
    second_0 = []
    for step in range(1, NY):
        there = moved(pos, "y", step)
        second_0.append(put(two_0.at[there["y"]], in_0.at[step - 1], device(there, core)))

    for copy in first_y:
        copy.wait_recv()
    for x in range(NX):
        value = total[1, pos["y"], x].astype(f32)
        for step in range(NY - 1):
            value += in_y[step, x].astype(f32)
        two_1[:, x] = value.astype(bf16)
    second_1 = []
    for step in range(1, NZ):
        there = moved(pos, "z", step)
        second_1.append(put(two_1.at[there["z"]], in_1.at[step - 1], device(there, core)))

    for copy in second_2:
        copy.wait_recv()
    value = two_2[:, pos["x"]].astype(f32)
    for step in range(NX - 1):
        value += in_2[step].astype(f32)
    last_2[...] = value.astype(bf16)
    third_2 = []
    for step in range(1, NY):
        there = moved(pos, "y", step)
        third_2.append(put(last_2.at[there["y"]], end_2.at[step - 1], device(there, core)))
    for copy in second_0:
        copy.wait_recv()
    value = two_0[pos["y"]].astype(f32)
    for step in range(NY - 1):
        value += in_0[step].astype(f32)
    last_0[...] = value.astype(bf16)
    third_0 = []
    for step in range(1, NZ):
        there = moved(pos, "z", step)
        third_0.append(put(last_0.at[there["z"]], end_0.at[step - 1], device(there, core)))
    for copy in second_1:
        copy.wait_recv()
    value = two_1[pos["z"]].astype(f32)
    for step in range(NZ - 1):
        value += in_1[step].astype(f32)
    last_1[...] = value.astype(bf16)
    third_1 = []
    for step in range(1, NX):
        there = moved(pos, "x", step)
        third_1.append(put(last_1.at[there["x"]], end_1.at[step - 1], device(there, core)))

    side_copy.wait_recv()
    ent_sum_ref[...] = ent_half[:, pl.ds(x_low, 1)][:, 0].astype(f32) + ent_side[...].astype(f32)

    for copies, lasts, ends, part, axis in (
        (third_2, last_2, end_2, 2, "y"),
        (third_0, last_0, end_0, 0, "z"),
        (third_1, last_1, end_1, 1, "x"),
    ):
        for copy in copies:
            copy.wait_recv()
        value = lasts[pos[axis]].astype(f32)
        for step in range(SIZES[axis] - 1):
            value += ends[step].astype(f32)
        rel_sum_ref[part] = value
    for copy in pending:
        copy.wait_send()


def scatter_sums(rel, ent):
    vmem = pl.BlockSpec(memory_space=pltpu.VMEM)
    tail = (SLOT, LANES)
    rows, width = ent.shape[3:]
    shapes = [
        (PARTS, NY, NX, NZ) + tail,
        (PARTS, NY, NX, NZ) + tail,
        (NX - 1, NY, NZ) + tail,
        (NY - 1, NX, NZ) + tail,
        (NZ - 1, NY, NX) + tail,
        (NZ - 1, NY, NX) + tail,
        (NY, NZ) + tail,
        (NY - 1, NZ) + tail,
        (NZ, NX) + tail,
        (NZ - 1, NX) + tail,
        (NY, NX) + tail,
        (NX - 1, NY) + tail,
        (NZ,) + tail,
        (NX,) + tail,
        (NY,) + tail,
        (NZ - 1,) + tail,
        (NX - 1,) + tail,
        (NY - 1,) + tail,
        (2, 2, rows, width),
        (2, 2, rows, width),
        (2, rows, width),
    ]
    return pl.pallas_call(
        scatter_kernel,
        out_shape=(
            jax.ShapeDtypeStruct((PARTS, SLOT, LANES), jnp.float32),
            jax.ShapeDtypeStruct((2, rows, width), jnp.float32),
        ),
        in_specs=[vmem] * 2,
        out_specs=(vmem, vmem),
        scratch_shapes=[pltpu.VMEM(shape, jnp.bfloat16) for shape in shapes]
        + [
            pltpu.SemaphoreType.DMA((SCATTER_COPIES,)),
            pltpu.SemaphoreType.DMA((SCATTER_COPIES,)),
        ],
        compiler_params=pltpu.CompilerParams(
            collective_id=1, has_side_effects=True, vmem_limit_bytes=VMEM_LIMIT
        ),
    )(rel, ent)


def replicas_kernel(piece_ref, whole_ref, send, recv):
    pos, core = here()
    sems = Sems(send, recv)
    x_low = lax.rem(pos["x"], 2)
    side = dict(pos)
    side["x"] = pos["x"] + 1 - 2 * x_low
    side_device, sibling = device(side, core), device(pos, 1 - core)
    whole_ref[x_low, core] = piece_ref[...]
    greet([side_device, sibling])
    mine = whole_ref.at[x_low, core]
    other = whole_ref.at[1 - x_low, core]
    copies = [sems.copy(mine, mine, side_device), sems.copy(mine, mine, sibling)]
    for copy in copies:
        copy.start()
    copies[0].wait_recv()
    last = sems.copy(other, other, sibling)
    last.start()
    copies[1].wait_recv()
    last.wait_recv()
    for copy in copies + [last]:
        copy.wait_send()


def gather_replicas(piece):
    vmem = pl.BlockSpec(memory_space=pltpu.VMEM)
    return pl.pallas_call(
        replicas_kernel,
        out_shape=jax.ShapeDtypeStruct((2, NC) + piece.shape, piece.dtype),
        in_specs=[vmem],
        out_specs=vmem,
        scratch_shapes=[pltpu.SemaphoreType.DMA((3,)), pltpu.SemaphoreType.DMA((3,))],
        compiler_params=pltpu.CompilerParams(collective_id=2, has_side_effects=True),
    )(piece)


def to_partner(piece, mask):
    count = lax.axis_size("dom")

    def branch(bits):
        route = [(low, low ^ bits) for low in range(count)]
        return lambda value: lax.ppermute(value, "dom", route)

    return lax.switch(mask - 1, [branch(bits) for bits in range(1, count)], piece)


def adagrad(param, state, grad):
    new_state = state + jnp.mean(grad * grad, axis=1)
    return (param - LEARN * grad / jnp.sqrt(new_state)[:, None], new_state)


def table_rows(ids, shard):
    owner, row = ids // shard, ids % shard
    dom, rep = owner // 4, owner % 4
    y, x, z = dom // (2 * NZ), (dom // NZ) % 2 * 2 + rep // 2, dom % NZ
    return ((((rep % 2) * NY + y) * NX + x) * NZ + z) * SLOT + row


def local(
    entities,
    entity_state,
    relations,
    relation_state,
    head_ids,
    relation_ids,
    tail_ids,
    head_negatives,
    tail_negatives,
    bucket_sizes,
    plan,
):
    ent_rows, width = entities.shape
    shard = relations.shape[0]
    edge_slots = head_ids.shape[0]
    blocks, samples = head_negatives.shape
    block_rows = edge_slots // blocks
    padded = -(-block_rows // TILE) * TILE
    rep_index = lax.axis_index("rep")
    piece_rows = ent_rows // 4
    own_low = entities.astype(jnp.bfloat16)
    own_piece = lax.dynamic_slice_in_dim(own_low, rep_index * piece_rows, piece_rows, 0)
    mask = plan[0]

    relation_low = jnp.pad(relations.astype(jnp.bfloat16), ((0, SLOT - shard), (0, 0)))
    relation_low = relation_low.reshape(SLOT, PARTS, LANES).transpose(1, 0, 2)
    table, partner = gather_tables(relation_low, to_partner(own_piece, mask))

    def lanes(values, fill):
        values = values.reshape(blocks, block_rows)
        values = jnp.pad(values, ((0, 0), (0, padded - block_rows)), constant_values=fill)
        return values.reshape(1, blocks * padded)

    slots = rep_index * edge_slots + jnp.arange(edge_slots, dtype=jnp.int32)
    active = (slots < bucket_sizes[0]).astype(jnp.float32)
    ids = jnp.concatenate(
        [lanes(head_ids, -1), lanes(table_rows(relation_ids, shard), -1), lanes(tail_ids, -1)],
        axis=0,
    )
    negs = jnp.pad(
        jnp.concatenate([head_negatives, tail_negatives], axis=0),
        ((0, 0), (0, -samples % LANES)),
        constant_values=-1,
    )
    head_sum, tail_sum, relation_part = compute(
        ids,
        lanes(active, 0.0),
        negs,
        own_low,
        partner.reshape(ent_rows, width),
        table.reshape(PARTS, ROWS, LANES),
        samples,
    )
    ent = jnp.stack([head_sum, tail_sum]).reshape(2, 2, NC, piece_rows, width)
    relation_sum, entity_part = scatter_sums(
        relation_part.reshape(PARTS, NC, NY, NX, NZ, SLOT, LANES), ent
    )
    returned = to_partner(entity_part[1].astype(jnp.bfloat16), mask)
    summed_piece = (entity_part[0] + returned.astype(jnp.float32)).astype(jnp.bfloat16)
    summed = gather_replicas(summed_piece).reshape(ent_rows, width).astype(jnp.float32)
    new_entities, new_entity_state = adagrad(entities, entity_state, summed)
    relation_sum = relation_sum.transpose(1, 0, 2).reshape(SLOT, width)[:shard]
    new_relations, new_relation_state = adagrad(relations, relation_state, relation_sum)
    return (new_entities, new_entity_state, new_relations, new_relation_state)


def solution(mesh):
    placed = (
        P("dom", None),
        P("dom"),
        P(("dom", "rep"), None),
        P(("dom", "rep")),
        P(("dom", "rep")),
        P(("dom", "rep")),
        P(("dom", "rep")),
        P(("dom", "rep"), None),
        P(("dom", "rep"), None),
        P("dom"),
        P(),
    )
    return jax.shard_map(
        local,
        mesh=mesh,
        in_specs=placed,
        out_specs=(P("dom", None), P("dom"), P(("dom", "rep"), None), P(("dom", "rep"))),
        check_vma=False,
    )
```

```python
import functools

import jax
import jax.numpy as jnp
from jax import lax
from jax.experimental import pallas as pl
from jax.experimental.pallas import tpu as pltpu
from jax.sharding import PartitionSpec as P

LEARN = 0.1
NX, NY, NZ, NC = 4, 4, 8, 2
SIZES = {"x": NX, "y": NY, "z": NZ}
PARTS, HALF = 2, 16
SECOND, LAST = ("y", "x"), ("x", "y")
FOUR = 4
MESH = pl.DeviceIdType.MESH
VMEM_LIMIT = 56 * 1024 * 1024
CHUNK = FOUR * NZ * HALF
TILE = 512
LANES = 128
INNER = (((1,), (1,)), ((), ()))
FIRST = (((0,), (0,)), ((), ()))


def here():
    dom = lax.axis_index("dom")
    rep = lax.axis_index("rep")
    pos = {
        "y": dom // (2 * NZ),
        "x": lax.rem(dom // NZ, 2) * 2 + rep // 2,
        "z": lax.rem(dom, NZ),
    }
    return pos, lax.rem(rep, 2)


def device(pos, core):
    dom = pos["y"] * (2 * NZ) + (pos["x"] // 2) * NZ + pos["z"]
    rep = lax.rem(pos["x"], 2) * 2 + core
    return (dom, rep)


def moved(pos, axis, offset):
    there = dict(pos)
    there[axis] = lax.rem(pos[axis] + offset + SIZES[axis], SIZES[axis])
    return there


def beside(pos):
    there = dict(pos)
    there["x"] = pos["x"] + 1 - 2 * lax.rem(pos["x"], 2)
    return there


def greet(devices):
    barrier = pltpu.get_barrier_semaphore()
    for target in devices:
        pl.semaphore_signal(barrier, inc=1, device_id=target, device_id_type=MESH)
    pl.semaphore_wait(barrier, len(devices))


def all_peers(pos, core):
    peers = [device(pos, 1 - core)]
    for axis, count in SIZES.items():
        peers += [device(moved(pos, axis, step), core) for step in range(1, count)]
    return peers


class Copies:
    def __init__(self, send, recv):
        self.send, self.recv, self.started = send, recv, []

    def put(self, source, target, device_id):
        index = len(self.started)
        copy = pltpu.make_async_remote_copy(
            src_ref=source,
            dst_ref=target,
            send_sem=self.send.at[index],
            recv_sem=self.recv.at[index],
            device_id=device_id,
            device_id_type=MESH,
        )
        copy.start()
        self.started.append(copy)
        return copy

    def finish(self):
        for copy in self.started:
            copy.wait_send()


class Partner:
    ORDERS = (("x", "y", "z"), ("z", "y", "x"))
    COUNTS = {"x": 2, "y": NY, "z": NZ}

    def __init__(self, copies, pos, core, mask, buffers):
        self.copies, self.pos, self.core, self.buffers = copies, pos, core, buffers
        self.index = {"x": pos["x"] // 2, "y": pos["y"], "z": pos["z"]}
        self.bits = {"x": mask // NZ % 2, "y": mask // (2 * NZ), "z": mask % NZ}
        self.flying = {}

    def send(self, half, stage, rows):
        axis = self.ORDERS[half][stage]
        slots = self.buffers[half][axis]
        mine = slots.at[self.index[axis]]
        mine[...] = rows
        steps = (2,) if axis == "x" else range(1, self.COUNTS[axis])
        self.flying[half, stage] = [
            self.copies.put(mine, mine, device(moved(self.pos, axis, step), self.core))
            for step in steps
        ]

    def take(self, half, stage):
        axis = self.ORDERS[half][stage]
        for copy in self.flying[half, stage]:
            copy.wait_recv()
        return self.buffers[half][axis][jnp.bitwise_xor(self.index[axis], self.bits[axis])]

    @classmethod
    def scratch(cls, rows, width):
        return [
            pltpu.VMEM((cls.COUNTS[axis], rows, width), jnp.bfloat16)
            for _ in cls.ORDERS
            for axis in ("x", "y", "z")
        ]

    @staticmethod
    def name(refs):
        return [dict(zip(("x", "y", "z"), refs[:3])), dict(zip(("x", "y", "z"), refs[3:6]))]


def dot(a, b, dims=(((1,), (0,)), ((), ()))):
    return lax.dot_general(a, b, dims, preferred_element_type=jnp.float32)


def one_hot(ids, base, count):
    rows = lax.broadcasted_iota(jnp.int32, (count, ids.shape[1]), 0)
    return jnp.where(rows == ids - base, 1.0, 0.0).astype(jnp.bfloat16)


def at_part(part, first, second):
    return first + part * (second - first)


def chunk_base(part, core, second):
    return ((part * NC + core) * FOUR + second) * CHUNK


GATHER_COPIES = 80


def gather_kernel(
    plan_ref, ids_ref, rel_ref, own_ref, w_ref, partner_ref, table, w_sum, *rest
):
    buffers, (send, recv) = Partner.name(rest[:6]), rest[6:]
    pos, core = here()
    copies = Copies(send, recv)
    put = copies.put
    sibling = device(pos, 1 - core)
    x_low = lax.rem(pos["x"], 2)
    rows = partner_ref.shape[2]
    for part in range(PARTS):
        table[part, core, pos[SECOND[part]], pos[LAST[part]], pos["z"]] = rel_ref[part]
    w_sum[...] = jnp.zeros_like(w_sum)
    greet(all_peers(pos, core))

    along_z = []
    for part in range(PARTS):
        mine = table.at[part, core, pos[SECOND[part]], pos[LAST[part]], pos["z"]]
        along_z += [
            put(mine, mine, device(moved(pos, "z", step), core)) for step in range(1, NZ)
        ]
    partner = Partner(copies, pos, core, plan_ref[0], buffers)
    first = pl.multiple_of((x_low * NC + core) * rows, rows)
    partner.send(0, 0, own_ref[pl.ds(first, rows // 2), :])
    partner.send(1, 0, own_ref[pl.ds(first + rows // 2, rows // 2), :])

    along_second, along_last = [], []
    for copy in along_z:
        copy.wait_recv()

    def spread(part, step):
        where = moved(pos, SECOND[part], -step)
        column = table.at[part, core, where[SECOND[part]], pos[LAST[part]]]
        return [
            put(column, column, device(moved(pos, LAST[part], there), core))
            for there in range(1, FOUR)
        ]

    for part in range(PARTS):
        column = table.at[part, core, pos[SECOND[part]], pos[LAST[part]]]
        along_second.append(
            [
                put(column, column, device(moved(pos, SECOND[part], step), core))
                for step in range(1, FOUR)
            ]
        )
    along_last.append([spread(part, 0) for part in range(PARTS)])
    partner.send(0, 1, partner.take(0, 0))

    def add(which, step):
        @pl.loop(0, PARTS)
        def _(part):
            second = lax.rem(at_part(part, pos["y"], pos["x"]) - step + FOUR, FOUR)
            block = table[part, which, second].reshape(CHUNK, table.shape[-1])
            hot = one_hot(ids_ref[1:2, :], chunk_base(part, which, second), CHUNK)
            w_sum[...] += dot(block, hot, FIRST)

    across = []

    def cross(step):
        chunks = []
        for part in range(PARTS):
            for copy in along_last[step][part]:
                copy.wait_recv()
            second = moved(pos, SECOND[part], -step)[SECOND[part]]
            chunk = table.at[part, core, second]
            chunks.append(put(chunk, chunk, sibling))
        across.append(chunks)

    def add_across(step):
        for copy in across[step]:
            copy.wait_recv()
        add(1 - core, step)

    for step in range(1, FOUR):
        for part in range(PARTS):
            along_second[part][step - 1].wait_recv()
        along_last.append([spread(part, step) for part in range(PARTS)])
    partner.send(1, 1, partner.take(1, 0))
    cross(0)
    partner.send(0, 2, partner.take(0, 1))
    add(core, 0)
    cross(1)
    add_across(0)
    partner.send(1, 2, partner.take(1, 1))
    cross(2)
    add(core, 1)
    add_across(1)
    mine = partner_ref.at[x_low, core]
    other = partner_ref.at[1 - x_low, core]
    mine[: rows // 2, :] = partner.take(0, 2)
    mine[rows // 2 :, :] = partner.take(1, 2)
    to_side = put(mine, mine, device(beside(pos), core))
    to_sibling = put(mine, mine, sibling)
    cross(3)
    add(core, 2)
    to_side.wait_recv()
    last = put(other, other, sibling)
    add_across(2)
    add(core, 3)
    add_across(3)
    w_ref[...] = w_sum[...].astype(jnp.bfloat16)
    to_sibling.wait_recv()
    last.wait_recv()
    copies.finish()


def vmem_spec():
    return pl.BlockSpec(memory_space=pltpu.VMEM)


def smem_spec():
    return pl.BlockSpec(memory_space=pltpu.SMEM)


def gather_rows(plan, ids, rel, own):
    width = own.shape[1]
    lanes = ids.shape[1]
    rows = own.shape[0] // 4
    return pl.pallas_call(
        gather_kernel,
        out_shape=(
            jax.ShapeDtypeStruct((width, lanes), jnp.bfloat16),
            jax.ShapeDtypeStruct((2, NC, rows, width), jnp.bfloat16),
        ),
        in_specs=[smem_spec()] + [vmem_spec()] * 3,
        out_specs=(vmem_spec(),) * 2,
        scratch_shapes=[
            pltpu.VMEM((PARTS, NC, FOUR, FOUR, NZ, HALF, width), jnp.bfloat16),
            pltpu.VMEM((width, lanes), jnp.float32),
        ]
        + Partner.scratch(rows // 2, width)
        + [pltpu.SemaphoreType.DMA((GATHER_COPIES,))] * 2,
        compiler_params=pltpu.CompilerParams(
            collective_id=0, has_side_effects=True, vmem_limit_bytes=VMEM_LIMIT
        ),
    )(plan, ids, rel, own)


def compute_kernel(
    block_rows,
    samples,
    live_ref,
    ids_ref,
    negs_ref,
    own_ref,
    par_ref,
    w_ref,
    ent_ref,
    rg_ref,
    own_t,
    par_t,
    count_ref,
    head_acc,
    tail_acc,
):
    bf16 = jnp.bfloat16
    ent = own_ref.shape[0]
    half = own_ref.shape[1] // 2
    lanes = ids_ref.shape[1]
    own_t[...] = own_ref[...].astype(jnp.float32).T.astype(bf16)
    par_t[...] = par_ref[...].astype(jnp.float32).T.astype(bf16)
    ones = jnp.ones((negs_ref.shape[1], LANES), bf16)
    for row in range(4):
        count_ref[row] = dot(one_hot(negs_ref[row : row + 1, :], 0, ent), ones)
    head_acc[...] = jnp.zeros_like(head_acc)
    tail_acc[...] = jnp.zeros_like(tail_acc)

    @pl.loop(0, lanes // TILE)
    def _(tile):
        base = pl.multiple_of(tile * TILE, TILE)
        cols = pl.ds(base, TILE)
        slot = lax.broadcasted_iota(jnp.int32, (1, TILE), 1) + base
        act = jnp.where(slot < live_ref[0], 1.0, 0.0)
        in_first = slot < block_rows
        hot_h = one_hot(ids_ref[0:1, cols], 0, ent)
        hot_t = one_hot(ids_ref[2:3, cols], 0, ent)
        h = dot(own_t[...], hot_h)
        t = dot(par_t[...], hot_t)
        w = w_ref[:, cols].astype(jnp.float32)
        ha, hb, ta, tb, wa, wb = h[:half], h[half:], t[:half], t[half:], w[:half], w[half:]
        query = jnp.concatenate([ha * wa - hb * wb, ha * wb + hb * wa], axis=0)
        probe = jnp.concatenate([wa * ta + wb * tb, wa * tb - wb * ta], axis=0)
        positive = jnp.sum(query * t, axis=0, keepdims=True)
        query_low = query.astype(bf16)
        probe_low = probe.astype(bf16)
        pos_weight = -act * jax.nn.sigmoid(-positive)
        scaling = act / samples

        def weights(scores, row):
            repeats = TILE // LANES
            count = jnp.where(
                in_first,
                jnp.concatenate([count_ref[row]] * repeats, axis=1),
                jnp.concatenate([count_ref[row + 1]] * repeats, axis=1),
            )
            return (jax.nn.sigmoid(scores) * scaling * count).astype(bf16)

        tail_w = weights(dot(par_ref[...], query_low), 2)
        head_w = weights(dot(own_ref[...], probe_low), 0)
        qg = pos_weight * t + dot(par_t[...], tail_w)
        pg = dot(own_t[...], head_w)
        qa, qb, pa, pb = qg[:half], qg[half:], pg[:half], pg[half:]
        head_grad = jnp.concatenate([qa * wa + qb * wb, qb * wa - qa * wb], axis=0)
        tail_grad = (
            jnp.concatenate([pa * wa - pb * wb, pa * wb + pb * wa], axis=0) + pos_weight * query
        )
        rel_grad = jnp.concatenate(
            [qa * ha + qb * hb + pa * ta + pb * tb, qb * ha - qa * hb + pa * tb - pb * ta], axis=0
        )
        rg_ref[cols, :] = rel_grad.T.astype(bf16)
        head_acc[...] += dot(head_w, probe_low, INNER) + dot(hot_h, head_grad.astype(bf16), INNER)
        tail_acc[...] += dot(tail_w, query_low, INNER) + dot(hot_t, tail_grad.astype(bf16), INNER)

    shape = ent_ref.shape[1:]
    ent_ref[0] = head_acc[...].astype(bf16).reshape(shape)
    ent_ref[1] = tail_acc[...].astype(bf16).reshape(shape)


def compute(live, ids, negs, own, par, w, block_rows, samples):
    ent, width = own.shape
    lanes = ids.shape[1]
    return pl.pallas_call(
        functools.partial(compute_kernel, block_rows, samples),
        out_shape=(
            jax.ShapeDtypeStruct((2, 2, NC, ent // 4, width), jnp.bfloat16),
            jax.ShapeDtypeStruct((lanes, width), jnp.bfloat16),
        ),
        in_specs=[smem_spec()] + [vmem_spec()] * 5,
        out_specs=(vmem_spec(),) * 2,
        scratch_shapes=[
            pltpu.VMEM((width, ent), jnp.bfloat16),
            pltpu.VMEM((width, ent), jnp.bfloat16),
            pltpu.VMEM((4, ent, LANES), jnp.float32),
            pltpu.VMEM((ent, width), jnp.float32),
            pltpu.VMEM((ent, width), jnp.float32),
        ],
        compiler_params=pltpu.CompilerParams(vmem_limit_bytes=VMEM_LIMIT),
    )(live, ids, negs, own, par, w)


SCATTER_COPIES = 80


def scatter_kernel(
    plan_ref,
    ids_ref,
    rg_ref,
    ent_ref,
    rel_sum_ref,
    ent_sum_ref,
    for_core,
    from_core,
    product,
    total,
    in_last,
    two,
    in_second,
    three,
    in_z,
    ent_core,
    ent_half,
    ent_side,
    *rest,
):
    f32, bf16 = jnp.float32, jnp.bfloat16
    buffers, (send, recv) = Partner.name(rest[:6]), rest[6:]
    pos, core = here()
    copies = Copies(send, recv)
    put = copies.put
    sibling = device(pos, 1 - core)
    x_low = lax.rem(pos["x"], 2)
    rows = ent_ref.shape[3]
    width = ent_ref.shape[4]
    greet(all_peers(pos, core))
    ent_copy = put(ent_ref.at[:, :, 1 - core], ent_core, sibling)

    def chunk(part, which, step):
        second = lax.rem(at_part(part, pos["y"], pos["x"]) + step, FOUR)
        hot = one_hot(ids_ref[1:2, :], chunk_base(part, which, second), CHUNK)
        return dot(hot, rg_ref[...])

    def for_sibling(step):
        @pl.loop(0, PARTS)
        def _(part):
            for_core[step, part] = chunk(part, 1 - core, step).astype(bf16)

        return put(for_core.at[step], from_core.at[step], sibling)

    def for_chips(step, core_copy):
        @pl.loop(0, PARTS)
        def _(part):
            product[part] = chunk(part, core, step)

        core_copy.wait_recv()

        @pl.loop(0, PARTS)
        def _(part):
            summed = product[part] + from_core[step, part].astype(f32)
            total[step, part] = summed.astype(bf16).reshape(total.shape[2:])

        flying = []
        for part in range(PARTS):
            for there in range(1, FOUR):
                target = moved(pos, LAST[part], there)
                flying.append(
                    put(
                        total.at[step, part, target[LAST[part]]],
                        in_last.at[step, part, there - 1],
                        device(target, core),
                    )
                )
        return flying

    def sum_last(step, part):
        value = total[step, part, pos[LAST[part]]].astype(f32)
        for there in range(FOUR - 1):
            value += in_last[step, part, there].astype(f32)
        return value

    def to_second(step, flying):
        for copy in flying:
            copy.wait_recv()
        started = []
        for part in range(PARTS):
            two[step - 1, part] = sum_last(step, part).astype(bf16)
            started.append(
                put(
                    two.at[step - 1, part],
                    in_second.at[step - 1, part],
                    device(moved(pos, SECOND[part], step), core),
                )
            )
        return started

    partner = Partner(copies, pos, core, plan_ref[0], buffers)
    core_copy = for_sibling(1)
    ent_copy.wait_recv()
    ent_half[...] = (ent_ref[:, :, core].astype(f32) + ent_core[...].astype(f32)).astype(bf16)
    side_copy = put(ent_half.at[:, 1 - x_low], ent_side, device(beside(pos), core))
    flying_1 = for_chips(1, core_copy)
    core_copy = for_sibling(2)
    side_copy.wait_recv()
    piece = (ent_half[1, x_low].astype(f32) + ent_side[1].astype(f32)).astype(bf16)
    partner.send(1, 0, piece[rows // 2 :])
    partner.send(0, 0, piece[: rows // 2])
    flying_2 = for_chips(2, core_copy)
    seconds = to_second(1, flying_1)
    partner.send(0, 1, partner.take(0, 0))
    core_copy = for_sibling(3)
    flying_3 = for_chips(3, core_copy)
    partner.send(0, 2, partner.take(0, 1))
    seconds += to_second(2, flying_2)
    core_copy = for_sibling(0)
    partner.send(1, 1, partner.take(1, 0))
    flying_0 = for_chips(0, core_copy)
    partner.send(1, 2, partner.take(1, 1))
    seconds += to_second(3, flying_3)
    for copy in flying_0:
        copy.wait_recv()
    own = [sum_last(0, part) for part in range(PARTS)]
    for copy in seconds:
        copy.wait_recv()
    last_z = []
    for part in range(PARTS):
        value = own[part]
        for step in range(FOUR - 1):
            value += in_second[step, part].astype(f32)
        three[part] = value.astype(bf16)
        for step in range(1, NZ):
            target = moved(pos, "z", step)
            last_z.append(
                put(three.at[part, target["z"]], in_z.at[part, step - 1], device(target, core))
            )
    mine = ent_sum_ref.at[x_low, core]
    other = ent_sum_ref.at[1 - x_low, core]
    held = ent_half[0, x_low].astype(f32) + ent_side[0].astype(f32)
    for half in (1, 0):
        part_rows = slice(half * (rows // 2), (half + 1) * (rows // 2))
        mine[part_rows, :] = (held[part_rows] + partner.take(half, 2).astype(f32)).astype(bf16)
    to_side = put(mine, mine, device(beside(pos), core))
    to_sibling = put(mine, mine, sibling)
    to_side.wait_recv()
    last = put(other, other, sibling)
    for copy in last_z:
        copy.wait_recv()
    for part in range(PARTS):
        value = three[part, pos["z"]].astype(f32)
        for step in range(NZ - 1):
            value += in_z[part, step].astype(f32)
        rel_sum_ref[part] = value
    to_sibling.wait_recv()
    last.wait_recv()
    copies.finish()


def scatter_sums(plan, ids, rg, ent):
    rows, width = ent.shape[3:]
    bf16 = jnp.bfloat16
    column = (NZ, HALF, width)
    return pl.pallas_call(
        scatter_kernel,
        out_shape=(
            jax.ShapeDtypeStruct((PARTS, HALF, width), jnp.float32),
            jax.ShapeDtypeStruct((2, NC, rows, width), bf16),
        ),
        in_specs=[smem_spec()] + [vmem_spec()] * 3,
        out_specs=(vmem_spec(),) * 2,
        scratch_shapes=[
            pltpu.VMEM((FOUR, PARTS, CHUNK, width), bf16),
            pltpu.VMEM((FOUR, PARTS, CHUNK, width), bf16),
            pltpu.VMEM((PARTS, CHUNK, width), jnp.float32),
            pltpu.VMEM((FOUR, PARTS, FOUR) + column, bf16),
            pltpu.VMEM((FOUR, PARTS, FOUR - 1) + column, bf16),
            pltpu.VMEM((FOUR - 1, PARTS) + column, bf16),
            pltpu.VMEM((FOUR - 1, PARTS) + column, bf16),
            pltpu.VMEM((PARTS,) + column, bf16),
            pltpu.VMEM((PARTS, NZ - 1, HALF, width), bf16),
            pltpu.VMEM((2, 2, rows, width), bf16),
            pltpu.VMEM((2, 2, rows, width), bf16),
            pltpu.VMEM((2, rows, width), bf16),
        ]
        + Partner.scratch(rows // 2, width)
        + [pltpu.SemaphoreType.DMA((SCATTER_COPIES,))] * 2,
        compiler_params=pltpu.CompilerParams(
            collective_id=1, has_side_effects=True, vmem_limit_bytes=VMEM_LIMIT
        ),
    )(plan, ids, rg, ent)


def adagrad(param, state, grad):
    new_state = state + jnp.mean(grad * grad, axis=1)
    return (param - LEARN * grad / jnp.sqrt(new_state)[:, None], new_state)


def table_rows(ids, shard):
    owner, row = ids // shard, ids % shard
    dom, rep = owner // 4, owner % 4
    y, x, z = dom // (2 * NZ), (dom // NZ) % 2 * 2 + rep // 2, dom % NZ
    part = row // HALF
    second, last = at_part(part, y, x), at_part(part, x, y)
    return (((part * NC + rep % 2) * FOUR + second) * FOUR + last) * NZ * HALF + (
        z * HALF + row % HALF
    )


def local(
    entities,
    entity_state,
    relations,
    relation_state,
    head_ids,
    relation_ids,
    tail_ids,
    head_negatives,
    tail_negatives,
    bucket_sizes,
    plan,
):
    ent_rows, width = entities.shape
    shard = relations.shape[0]
    edge_slots = head_ids.shape[0]
    samples = head_negatives.shape[1]
    padded = -(-edge_slots // TILE) * TILE
    own_low = entities.astype(jnp.bfloat16)
    relation_low = jnp.pad(
        relations.astype(jnp.bfloat16), ((0, PARTS * HALF - shard), (0, 0))
    ).reshape(PARTS, HALF, width)
    ids = jnp.pad(
        jnp.stack([head_ids, table_rows(relation_ids, shard), tail_ids]),
        ((0, 0), (0, padded - edge_slots)),
        constant_values=-1,
    )
    live = jnp.minimum(bucket_sizes - lax.axis_index("rep") * edge_slots, edge_slots)
    negs = jnp.pad(
        jnp.concatenate([head_negatives, tail_negatives], axis=0),
        ((0, 0), (0, -samples % LANES)),
        constant_values=-1,
    )
    w, partner = gather_rows(plan, ids, relation_low, own_low)
    ent, rg = compute(
        live,
        ids,
        negs,
        own_low,
        partner.reshape(ent_rows, width),
        w,
        edge_slots // head_negatives.shape[0],
        samples,
    )
    relation_sum, summed = scatter_sums(plan, ids, rg, ent)
    summed = summed.reshape(ent_rows, width).astype(jnp.float32)
    new_entities, new_entity_state = adagrad(entities, entity_state, summed)
    relation_sum = relation_sum.reshape(PARTS * HALF, width)[:shard]
    new_relations, new_relation_state = adagrad(relations, relation_state, relation_sum)
    return (new_entities, new_entity_state, new_relations, new_relation_state)


def solution(mesh):
    placed = (
        P("dom", None),
        P("dom"),
        P(("dom", "rep"), None),
        P(("dom", "rep")),
        P(("dom", "rep")),
        P(("dom", "rep")),
        P(("dom", "rep")),
        P(("dom", "rep"), None),
        P(("dom", "rep"), None),
        P("dom"),
        P(),
    )
    return jax.shard_map(
        local,
        mesh=mesh,
        in_specs=placed,
        out_specs=(P("dom", None), P("dom"), P(("dom", "rep"), None), P(("dom", "rep"))),
        check_vma=False,
    )
```

```python
import functools

import jax
import jax.numpy as jnp
from jax import lax
from jax.experimental import pallas as pl
from jax.experimental.pallas import tpu as pltpu
from jax.sharding import PartitionSpec as P

LEARN = 0.1
NX, NY, NZ, NC = 4, 4, 8, 2
SIZES = {"x": NX, "y": NY, "z": NZ}
PARTS, HALF = 2, 16
SECOND, LAST = ("y", "x"), ("x", "y")
FOUR = 4
MESH = pl.DeviceIdType.MESH
VMEM_LIMIT = 56 * 1024 * 1024
CHUNK = FOUR * NZ * HALF
TILE = 512
LANES = 128
INNER = (((1,), (1,)), ((), ()))
FIRST = (((0,), (0,)), ((), ()))


def here():
    dom = lax.axis_index("dom")
    rep = lax.axis_index("rep")
    pos = {
        "y": dom // (2 * NZ),
        "x": lax.rem(dom // NZ, 2) * 2 + rep // 2,
        "z": lax.rem(dom, NZ),
    }
    return pos, lax.rem(rep, 2)


def device(pos, core):
    dom = pos["y"] * (2 * NZ) + (pos["x"] // 2) * NZ + pos["z"]
    rep = lax.rem(pos["x"], 2) * 2 + core
    return (dom, rep)


def moved(pos, axis, offset):
    there = dict(pos)
    there[axis] = lax.rem(pos[axis] + offset + SIZES[axis], SIZES[axis])
    return there


def beside(pos):
    there = dict(pos)
    there["x"] = pos["x"] + 1 - 2 * lax.rem(pos["x"], 2)
    return there


def signal_all(devices):
    barrier = pltpu.get_barrier_semaphore()
    for target in devices:
        pl.semaphore_signal(barrier, inc=1, device_id=target, device_id_type=MESH)


def wait_all(devices):
    pl.semaphore_wait(pltpu.get_barrier_semaphore(), len(devices))


def all_peers(pos, core):
    peers = [device(pos, 1 - core), device(beside(pos), 1 - core)]
    for axis, count in SIZES.items():
        peers += [device(moved(pos, axis, step), core) for step in range(1, count)]
    return peers


COPIES = 144


class Copies:
    def __init__(self, send, recv):
        self.send, self.recv, self.started = send, recv, []

    def put(self, source, target, device_id):
        index = len(self.started)
        assert index < COPIES
        copy = pltpu.make_async_remote_copy(
            src_ref=source,
            dst_ref=target,
            send_sem=self.send.at[index],
            recv_sem=self.recv.at[index],
            device_id=device_id,
            device_id_type=MESH,
        )
        copy.start()
        self.started.append(copy)
        return copy

    def finish(self):
        for copy in self.started:
            copy.wait_send()


class Partner:
    COUNTS = {"x": 2, "y": NY, "z_hi": NZ // 2, "z_lo": 2}

    def __init__(self, copies, pos, core, mask, refs):
        self.copies, self.pos, self.core = copies, pos, core
        names = list(self.COUNTS)
        self.buffers = [dict(zip(names, refs[:4])), dict(zip(names, refs[4:8]))]
        self.index = {
            "x": pos["x"] // 2,
            "y": pos["y"],
            "z_hi": pos["z"] // 2,
            "z_lo": lax.rem(pos["z"], 2),
        }
        self.bits = {
            "x": mask // NZ % 2,
            "y": mask // (2 * NZ),
            "z_hi": mask % NZ // 2,
            "z_lo": mask % 2,
        }
        self.flying = {}

    def peers(self, axis):
        pos = self.pos
        if axis == "x":
            return [moved(pos, "x", 2)]
        if axis == "y":
            return [moved(pos, "y", step) for step in range(1, NY)]
        if axis == "z_hi":
            return [moved(pos, "z", step) for step in range(2, NZ, 2)]
        return [moved(pos, "z", 1 - 2 * self.index["z_lo"])]

    def send(self, half, axis, rows):
        mine = self.buffers[half][axis].at[self.index[axis]]
        mine[...] = rows
        self.flying[half, axis] = [
            self.copies.put(mine, mine, device(there, self.core)) for there in self.peers(axis)
        ]

    def take(self, half, axis):
        for copy in self.flying[half, axis]:
            copy.wait_recv()
        return self.buffers[half][axis][jnp.bitwise_xor(self.index[axis], self.bits[axis])]

    def turn(self, axis, following):
        for half in range(2):
            self.send(half, following, self.take(half, axis))

    @classmethod
    def scratch(cls, rows, width):
        return [
            pltpu.VMEM((count, rows, width), jnp.bfloat16)
            for _ in range(2)
            for count in cls.COUNTS.values()
        ]


def to_replicas(put, whole, pos, core):
    mine = whole.at[lax.rem(pos["x"], 2), core]
    others = [device(beside(pos), core), device(beside(pos), 1 - core), device(pos, 1 - core)]
    return [put(mine, mine, target) for target in others]


def dot(a, b, dims=(((1,), (0,)), ((), ()))):
    return lax.dot_general(a, b, dims, preferred_element_type=jnp.float32)


def one_hot(ids, base, count):
    rows = lax.broadcasted_iota(jnp.int32, (count, ids.shape[1]), 0)
    return jnp.where(rows == ids - base, 1.0, 0.0).astype(jnp.bfloat16)


def at_part(part, first, second):
    return first + part * (second - first)


def chunk_base(part, core, second):
    return ((part * NC + core) * FOUR + second) * CHUNK


class Scratch:
    def __init__(self, ent, width, lanes, samples):
        rows = ent // 4
        bf16, f32 = jnp.bfloat16, jnp.float32
        column = (NZ, HALF, width)
        vmem = pltpu.VMEM
        self.shapes = {
            "ids": vmem((3, lanes), jnp.int32),
            "negs": vmem((4, -(-samples // LANES) * LANES), jnp.int32),
            "rel": vmem((PARTS * HALF, width), f32),
            "table": vmem((PARTS, NC, FOUR, FOUR) + column, bf16),
            "partner": vmem((2, NC, rows, width), bf16),
            "own": vmem((ent, width), bf16),
            "own_t": vmem((width, ent), bf16),
            "par_t": vmem((width, ent), bf16),
            "count": vmem((4, ent, LANES), f32),
            "h": vmem((width, lanes), bf16),
            "t": vmem((width, lanes), bf16),
            "w": vmem((width, lanes), f32),
            "head": vmem((ent, width), f32),
            "tail": vmem((ent, width), f32),
            "rg": vmem((lanes, width), bf16),
            "ent": vmem((2, 2, NC, rows, width), bf16),
            "for_core": vmem((FOUR, PARTS, CHUNK, width), bf16),
            "from_core": vmem((FOUR, PARTS, CHUNK, width), bf16),
            "product": vmem((PARTS, CHUNK, width), f32),
            "total": vmem((FOUR, PARTS, FOUR) + column, bf16),
            "in_last": vmem((FOUR, PARTS, FOUR - 1) + column, bf16),
            "two": vmem((FOUR - 1, PARTS) + column, bf16),
            "in_second": vmem((FOUR - 1, PARTS) + column, bf16),
            "three": vmem((PARTS,) + column, bf16),
            "in_z": vmem((PARTS, NZ - 1, HALF, width), bf16),
            "ent_core": vmem((2, 2, rows, width), bf16),
            "ent_half": vmem((2, 2, rows, width), bf16),
            "ent_side": vmem((2, rows, width), bf16),
            "send": pltpu.SemaphoreType.DMA((COPIES,)),
            "recv": pltpu.SemaphoreType.DMA((COPIES,)),
        }
        self.partner = Partner.scratch(rows // 2, width)

    def types(self):
        return list(self.shapes.values()) + self.partner + self.partner

    def bind(self, refs):
        for name, ref in zip(self.shapes, refs):
            setattr(self, name, ref)
        rest = refs[len(self.shapes) :]
        self.there, self.back = rest[:8], rest[8:]


def round_kernel(scratch, block_rows, samples, *refs):
    plan_ref, live_ref, ids_in, head_negs, tail_negs, rel_in, own_in = refs[:7]
    rel_sum_ref, ent_sum_ref = refs[7:9]
    v = scratch
    v.bind(refs[9:])
    f32, bf16 = jnp.float32, jnp.bfloat16
    pos, core = here()
    copies = Copies(v.send, v.recv)
    put = copies.put
    sibling = device(pos, 1 - core)
    x_low = lax.rem(pos["x"], 2)
    ent, width = own_in.shape
    half = width // 2
    rows = ent // 4
    lanes = v.w.shape[1]
    peers = all_peers(pos, core)

    signal_all(peers)
    shard = rel_in.shape[0]
    v.rel[...] = jnp.zeros_like(v.rel)
    v.rel[:shard, :] = rel_in[...]
    for part in range(PARTS):
        slot = v.table.at[part, core, pos[SECOND[part]], pos[LAST[part]], pos["z"]]
        slot[...] = v.rel[part * HALF : (part + 1) * HALF, :].astype(bf16)
    v.own[...] = own_in[...].astype(bf16)
    wait_all(peers)

    along_z = []
    for part in range(PARTS):
        mine = v.table.at[part, core, pos[SECOND[part]], pos[LAST[part]], pos["z"]]
        along_z += [
            put(mine, mine, device(moved(pos, "z", step), core)) for step in range(1, NZ)
        ]
    partner = Partner(copies, pos, core, plan_ref[0], v.there)
    first = pl.multiple_of((x_low * NC + core) * rows, rows)
    for side in range(2):
        partner.send(side, "x", v.own[pl.ds(first + side * (rows // 2), rows // 2), :])

    v.ids[...] = jnp.full_like(v.ids, -1)
    v.ids[:, : ids_in.shape[1]] = ids_in[...]
    v.negs[...] = jnp.full_like(v.negs, -1)
    v.negs[0:2, :samples] = head_negs[...]
    v.negs[2:4, :samples] = tail_negs[...]
    v.own_t[...] = v.own[...].astype(f32).T.astype(bf16)
    v.w[...] = jnp.zeros_like(v.w)
    v.head[...] = jnp.zeros_like(v.head)
    v.tail[...] = jnp.zeros_like(v.tail)
    partner.turn("x", "y")
    for copy in along_z:
        copy.wait_recv()

    along_second, along_last = [], []

    def spread(part, step):
        where = moved(pos, SECOND[part], -step)
        column = v.table.at[part, core, where[SECOND[part]], pos[LAST[part]]]
        return [
            put(column, column, device(moved(pos, LAST[part], there), core))
            for there in range(1, FOUR)
        ]

    for part in range(PARTS):
        column = v.table.at[part, core, pos[SECOND[part]], pos[LAST[part]]]
        along_second.append(
            [
                put(column, column, device(moved(pos, SECOND[part], step), core))
                for step in range(1, FOUR)
            ]
        )
    along_last.append([spread(part, 0) for part in range(PARTS)])
    partner.turn("y", "z_hi")
    for step in range(1, FOUR):
        for part in range(PARTS):
            along_second[part][step - 1].wait_recv()
        along_last.append([spread(part, step) for part in range(PARTS)])

    def tiles(body):
        @pl.loop(0, lanes // TILE)
        def _(tile):
            base = pl.multiple_of(tile * TILE, TILE)
            body(base, pl.ds(base, TILE))

    def gather_heads(base, cols):
        v.h[:, cols] = dot(v.own_t[...], one_hot(v.ids[0:1, cols], 0, ent)).astype(bf16)

    def gather_tails(base, cols):
        v.t[:, cols] = dot(v.par_t[...], one_hot(v.ids[2:3, cols], 0, ent)).astype(bf16)

    def add(which, step):
        @pl.loop(0, PARTS)
        def _(part):
            second = lax.rem(at_part(part, pos["y"], pos["x"]) - step + FOUR, FOUR)
            block = v.table[part, which, second].reshape(CHUNK, width)
            hot = one_hot(v.ids[1:2, :], chunk_base(part, which, second), CHUNK)
            v.w[...] += dot(block, hot, FIRST)

    across = []

    def cross(step):
        chunks = []
        for part in range(PARTS):
            for copy in along_last[step][part]:
                copy.wait_recv()
            second = moved(pos, SECOND[part], -step)[SECOND[part]]
            chunk = v.table.at[part, core, second]
            chunks.append(put(chunk, chunk, sibling))
        across.append(chunks)

    def add_across(step):
        for copy in across[step]:
            copy.wait_recv()
        add(1 - core, step)

    tiles(gather_heads)
    ones = jnp.ones((v.negs.shape[1], LANES), bf16)
    for row in range(4):
        v.count[row] = dot(one_hot(v.negs[row : row + 1, :], 0, ent), ones)
    cross(0)
    partner.turn("z_hi", "z_lo")
    add(core, 0)
    cross(1)
    mine = v.partner.at[x_low, core]
    mine[: rows // 2, :] = partner.take(0, "z_lo")
    mine[rows // 2 :, :] = partner.take(1, "z_lo")
    replicas = to_replicas(put, v.partner, pos, core)
    add_across(0)
    cross(2)
    add(core, 1)
    add_across(1)
    cross(3)
    add(core, 2)
    for copy in replicas:
        copy.wait_recv()
    v.par_t[...] = v.partner[...].reshape(ent, width).astype(f32).T.astype(bf16)
    tiles(gather_tails)
    add_across(2)
    add(core, 3)
    add_across(3)

    def edges(base, cols):
        slot = lax.broadcasted_iota(jnp.int32, (1, TILE), 1) + base
        act = jnp.where(slot < live_ref[0], 1.0, 0.0)
        in_first = slot < block_rows
        par = v.partner[...].reshape(ent, width)
        h, t, w = v.h[:, cols].astype(f32), v.t[:, cols].astype(f32), v.w[:, cols]
        ha, hb, ta, tb, wa, wb = h[:half], h[half:], t[:half], t[half:], w[:half], w[half:]
        query = jnp.concatenate([ha * wa - hb * wb, ha * wb + hb * wa], axis=0)
        probe = jnp.concatenate([wa * ta + wb * tb, wa * tb - wb * ta], axis=0)
        positive = jnp.sum(query * t, axis=0, keepdims=True)
        query_low = query.astype(bf16)
        probe_low = probe.astype(bf16)
        pos_weight = -act * jax.nn.sigmoid(-positive)
        scaling = act / samples

        def weights(scores, row):
            repeats = TILE // LANES
            count = jnp.where(
                in_first,
                jnp.concatenate([v.count[row]] * repeats, axis=1),
                jnp.concatenate([v.count[row + 1]] * repeats, axis=1),
            )
            return (jax.nn.sigmoid(scores) * scaling * count).astype(bf16)

        tail_w = weights(dot(par, query_low), 2)
        head_w = weights(dot(v.own[...], probe_low), 0)
        qg = pos_weight * t + dot(v.par_t[...], tail_w)
        pg = dot(v.own_t[...], head_w)
        qa, qb, pa, pb = qg[:half], qg[half:], pg[:half], pg[half:]
        head_grad = jnp.concatenate([qa * wa + qb * wb, qb * wa - qa * wb], axis=0)
        tail_grad = (
            jnp.concatenate([pa * wa - pb * wb, pa * wb + pb * wa], axis=0) + pos_weight * query
        )
        rel_grad = jnp.concatenate(
            [qa * ha + qb * hb + pa * ta + pb * tb, qb * ha - qa * hb + pa * tb - pb * ta], axis=0
        )
        v.rg[cols, :] = rel_grad.T.astype(bf16)
        hot_h = one_hot(v.ids[0:1, cols], 0, ent)
        hot_t = one_hot(v.ids[2:3, cols], 0, ent)
        v.head[...] += dot(head_w, probe_low, INNER) + dot(hot_h, head_grad.astype(bf16), INNER)
        v.tail[...] += dot(tail_w, query_low, INNER) + dot(hot_t, tail_grad.astype(bf16), INNER)

    tiles(edges)
    shape = v.ent.shape[1:]
    v.ent[0] = v.head[...].astype(bf16).reshape(shape)
    v.ent[1] = v.tail[...].astype(bf16).reshape(shape)

    ent_copy = put(v.ent.at[:, :, 1 - core], v.ent_core, sibling)

    def chunk(part, which, step):
        second = lax.rem(at_part(part, pos["y"], pos["x"]) + step, FOUR)
        hot = one_hot(v.ids[1:2, :], chunk_base(part, which, second), CHUNK)
        return dot(hot, v.rg[...])

    def for_sibling(step):
        @pl.loop(0, PARTS)
        def _(part):
            v.for_core[step, part] = chunk(part, 1 - core, step).astype(bf16)

        return put(v.for_core.at[step], v.from_core.at[step], sibling)

    def for_chips(step, core_copy):
        @pl.loop(0, PARTS)
        def _(part):
            v.product[part] = chunk(part, core, step)

        core_copy.wait_recv()

        @pl.loop(0, PARTS)
        def _(part):
            summed = v.product[part] + v.from_core[step, part].astype(f32)
            v.total[step, part] = summed.astype(bf16).reshape(v.total.shape[2:])

        flying = []
        for part in range(PARTS):
            for there in range(1, FOUR):
                target = moved(pos, LAST[part], there)
                flying.append(
                    put(
                        v.total.at[step, part, target[LAST[part]]],
                        v.in_last.at[step, part, there - 1],
                        device(target, core),
                    )
                )
        return flying

    def sum_last(step, part):
        value = v.total[step, part, pos[LAST[part]]].astype(f32)
        for there in range(FOUR - 1):
            value += v.in_last[step, part, there].astype(f32)
        return value

    def to_second(step, flying):
        for copy in flying:
            copy.wait_recv()
        started = []
        for part in range(PARTS):
            v.two[step - 1, part] = sum_last(step, part).astype(bf16)
            started.append(
                put(
                    v.two.at[step - 1, part],
                    v.in_second.at[step - 1, part],
                    device(moved(pos, SECOND[part], step), core),
                )
            )
        return started

    partner = Partner(copies, pos, core, plan_ref[0], v.back)
    core_copy = for_sibling(1)
    ent_copy.wait_recv()
    v.ent_half[...] = (v.ent[:, :, core].astype(f32) + v.ent_core[...].astype(f32)).astype(bf16)
    side_copy = put(v.ent_half.at[:, 1 - x_low], v.ent_side, device(beside(pos), core))
    flying_1 = for_chips(1, core_copy)
    core_copy = for_sibling(2)
    side_copy.wait_recv()
    piece = (v.ent_half[1, x_low].astype(f32) + v.ent_side[1].astype(f32)).astype(bf16)
    partner.send(0, "z_hi", piece[: rows // 2])
    partner.send(1, "z_hi", piece[rows // 2 :])
    flying_2 = for_chips(2, core_copy)
    seconds = to_second(1, flying_1)
    core_copy = for_sibling(3)
    partner.turn("z_hi", "z_lo")
    flying_3 = for_chips(3, core_copy)
    seconds += to_second(2, flying_2)
    partner.turn("z_lo", "y")
    core_copy = for_sibling(0)
    flying_0 = for_chips(0, core_copy)
    partner.turn("y", "x")
    seconds += to_second(3, flying_3)
    for copy in flying_0:
        copy.wait_recv()
    own = [sum_last(0, part) for part in range(PARTS)]
    for copy in seconds:
        copy.wait_recv()
    last_z = []
    for part in range(PARTS):
        value = own[part]
        for step in range(FOUR - 1):
            value += v.in_second[step, part].astype(f32)
        v.three[part] = value.astype(bf16)
        for step in range(1, NZ):
            target = moved(pos, "z", step)
            last_z.append(
                put(
                    v.three.at[part, target["z"]],
                    v.in_z.at[part, step - 1],
                    device(target, core),
                )
            )
    mine = ent_sum_ref.at[x_low, core]
    held = v.ent_half[0, x_low].astype(f32) + v.ent_side[0].astype(f32)
    for side in range(2):
        some = slice(side * (rows // 2), (side + 1) * (rows // 2))
        mine[some, :] = (held[some] + partner.take(side, "x").astype(f32)).astype(bf16)
    replicas = to_replicas(put, ent_sum_ref, pos, core)
    for copy in last_z:
        copy.wait_recv()
    for part in range(PARTS):
        value = v.three[part, pos["z"]].astype(f32)
        for step in range(NZ - 1):
            value += v.in_z[part, step].astype(f32)
        rel_sum_ref[part] = value
    for copy in replicas:
        copy.wait_recv()
    copies.finish()


def whole_round(plan, live, ids, head_negs, tail_negs, rel, own, block_rows):
    ent, width = own.shape
    samples = head_negs.shape[1]
    lanes = -(-ids.shape[1] // TILE) * TILE
    scratch = Scratch(ent, width, lanes, samples)
    smem = pl.BlockSpec(memory_space=pltpu.SMEM)
    vmem = pl.BlockSpec(memory_space=pltpu.VMEM)
    return pl.pallas_call(
        functools.partial(round_kernel, scratch, block_rows, samples),
        out_shape=(
            jax.ShapeDtypeStruct((PARTS, HALF, width), jnp.float32),
            jax.ShapeDtypeStruct((2, NC, ent // 4, width), jnp.bfloat16),
        ),
        in_specs=[smem] * 2 + [vmem] * 5,
        out_specs=(vmem,) * 2,
        scratch_shapes=scratch.types(),
        compiler_params=pltpu.CompilerParams(
            collective_id=0, has_side_effects=True, vmem_limit_bytes=VMEM_LIMIT
        ),
    )(plan, live, ids, head_negs, tail_negs, rel, own)


def adagrad(param, state, grad):
    new_state = state + jnp.mean(grad * grad, axis=1)
    return (param - LEARN * grad / jnp.sqrt(new_state)[:, None], new_state)


def table_rows(ids, shard):
    owner, row = ids // shard, ids % shard
    dom, rep = owner // 4, owner % 4
    y, x, z = dom // (2 * NZ), (dom // NZ) % 2 * 2 + rep // 2, dom % NZ
    part = row // HALF
    second, last = at_part(part, y, x), at_part(part, x, y)
    return (((part * NC + rep % 2) * FOUR + second) * FOUR + last) * NZ * HALF + (
        z * HALF + row % HALF
    )


def local(
    entities,
    entity_state,
    relations,
    relation_state,
    head_ids,
    relation_ids,
    tail_ids,
    head_negatives,
    tail_negatives,
    bucket_sizes,
    plan,
):
    ent_rows, width = entities.shape
    shard = relations.shape[0]
    edge_slots = head_ids.shape[0]
    ids = jnp.stack([head_ids, table_rows(relation_ids, shard), tail_ids])
    live = jnp.minimum(bucket_sizes - lax.axis_index("rep") * edge_slots, edge_slots)
    relation_sum, summed = whole_round(
        plan,
        live,
        ids,
        head_negatives,
        tail_negatives,
        relations,
        entities,
        edge_slots // head_negatives.shape[0],
    )
    summed = summed.reshape(ent_rows, width).astype(jnp.float32)
    new_entities, new_entity_state = adagrad(entities, entity_state, summed)
    relation_sum = relation_sum.reshape(PARTS * HALF, width)[:shard]
    new_relations, new_relation_state = adagrad(relations, relation_state, relation_sum)
    return (new_entities, new_entity_state, new_relations, new_relation_state)


def solution(mesh):
    placed = (
        P("dom", None),
        P("dom"),
        P(("dom", "rep"), None),
        P(("dom", "rep")),
        P(("dom", "rep")),
        P(("dom", "rep")),
        P(("dom", "rep")),
        P(("dom", "rep"), None),
        P(("dom", "rep"), None),
        P("dom"),
        P(),
    )
    return jax.shard_map(
        local,
        mesh=mesh,
        in_specs=placed,
        out_specs=(P("dom", None), P("dom"), P(("dom", "rep"), None), P(("dom", "rep"))),
        check_vma=False,
    )
```

```python
import functools

import jax
import jax.numpy as jnp
from jax import lax
from jax.experimental import pallas as pl
from jax.experimental.pallas import tpu as pltpu
from jax.sharding import PartitionSpec as P

LEARN = 0.1
NX, NY, NZ, NC = 4, 4, 8, 2
SIZES = {"x": NX, "y": NY, "z": NZ}
PARTS, HALF = 2, 16
SECOND, LAST = ("y", "x"), ("x", "y")
FOUR = 4
MESH = pl.DeviceIdType.MESH
VMEM_LIMIT = 56 * 1024 * 1024
COLUMN = NZ * HALF
CHUNK = FOUR * COLUMN
TILE = 512
LANES = 128
INNER = (((1,), (1,)), ((), ()))
FIRST = (((0,), (0,)), ((), ()))


def here():
    dom = lax.axis_index("dom")
    rep = lax.axis_index("rep")
    pos = {
        "y": dom // (2 * NZ),
        "x": lax.rem(dom // NZ, 2) * 2 + rep // 2,
        "z": lax.rem(dom, NZ),
    }
    return pos, lax.rem(rep, 2)


def device(pos, core):
    dom = pos["y"] * (2 * NZ) + (pos["x"] // 2) * NZ + pos["z"]
    rep = lax.rem(pos["x"], 2) * 2 + core
    return (dom, rep)


def moved(pos, axis, offset):
    there = dict(pos)
    there[axis] = lax.rem(pos[axis] + offset + SIZES[axis], SIZES[axis])
    return there


def beside(pos):
    there = dict(pos)
    there["x"] = pos["x"] + 1 - 2 * lax.rem(pos["x"], 2)
    return there


def signal_all(devices):
    barrier = pltpu.get_barrier_semaphore()
    for target in devices:
        pl.semaphore_signal(barrier, inc=1, device_id=target, device_id_type=MESH)


def wait_all(devices):
    pl.semaphore_wait(pltpu.get_barrier_semaphore(), len(devices))


def all_peers(pos, core):
    peers = [device(pos, 1 - core), device(beside(pos), 1 - core)]
    for axis, count in SIZES.items():
        peers += [device(moved(pos, axis, step), core) for step in range(1, count)]
    return peers


COPIES = 176


class Copies:
    def __init__(self, send, recv):
        self.send, self.recv, self.started = send, recv, []

    def put(self, source, target, device_id):
        index = len(self.started)
        assert index < COPIES
        copy = pltpu.make_async_remote_copy(
            src_ref=source,
            dst_ref=target,
            send_sem=self.send.at[index],
            recv_sem=self.recv.at[index],
            device_id=device_id,
            device_id_type=MESH,
        )
        copy.start()
        self.started.append(copy)
        return copy

    def finish(self):
        for copy in self.started:
            copy.wait_send()


class Partner:
    COUNTS = {"x": 2, "y": NY, "z_hi": NZ // 2, "z_lo": 2}

    def __init__(self, copies, pos, core, mask, refs):
        self.copies, self.pos, self.core = copies, pos, core
        names = list(self.COUNTS)
        self.buffers = [dict(zip(names, refs[:4])), dict(zip(names, refs[4:8]))]
        self.index = {
            "x": pos["x"] // 2,
            "y": pos["y"],
            "z_hi": pos["z"] // 2,
            "z_lo": lax.rem(pos["z"], 2),
        }
        self.bits = {
            "x": mask // NZ % 2,
            "y": mask // (2 * NZ),
            "z_hi": mask % NZ // 2,
            "z_lo": mask % 2,
        }
        self.flying = {}

    def peers(self, axis):
        pos = self.pos
        if axis == "x":
            return [moved(pos, "x", 2)]
        if axis == "y":
            return [moved(pos, "y", step) for step in range(1, NY)]
        if axis == "z_hi":
            return [moved(pos, "z", step) for step in range(2, NZ, 2)]
        return [moved(pos, "z", 1 - 2 * self.index["z_lo"])]

    def send(self, half, axis, rows):
        mine = self.buffers[half][axis].at[self.index[axis]]
        mine[...] = rows
        self.flying[half, axis] = [
            self.copies.put(mine, mine, device(there, self.core)) for there in self.peers(axis)
        ]

    def take(self, half, axis):
        for copy in self.flying[half, axis]:
            copy.wait_recv()
        return self.buffers[half][axis][jnp.bitwise_xor(self.index[axis], self.bits[axis])]

    def turn(self, axis, following):
        for half in range(2):
            self.send(half, following, self.take(half, axis))

    @classmethod
    def scratch(cls, rows, width):
        return [
            pltpu.VMEM((count, rows, width), jnp.bfloat16)
            for _ in range(2)
            for count in cls.COUNTS.values()
        ]


def to_replicas(put, whole, pos, core):
    mine = whole.at[lax.rem(pos["x"], 2), core]
    others = [device(beside(pos), core), device(beside(pos), 1 - core), device(pos, 1 - core)]
    return [put(mine, mine, target) for target in others]


def dot(a, b, dims=(((1,), (0,)), ((), ()))):
    return lax.dot_general(a, b, dims, preferred_element_type=jnp.float32)


def one_hot(ids, base, count):
    rows = lax.broadcasted_iota(jnp.int32, (count, ids.shape[1]), 0)
    return jnp.where(rows == ids - base, 1.0, 0.0).astype(jnp.bfloat16)


def at_part(part, first, second):
    return first + part * (second - first)


def chunk_base(part, core, second):
    return ((part * NC + core) * FOUR + second) * CHUNK


class Scratch:
    def __init__(self, ent, width, lanes, samples):
        rows = ent // 4
        bf16, f32 = jnp.bfloat16, jnp.float32
        column = (NZ, HALF, width)
        turned = (width, COLUMN)
        vmem = pltpu.VMEM
        self.shapes = {
            "ids": vmem((3, lanes), jnp.int32),
            "negs": vmem((4, -(-samples // LANES) * LANES), jnp.int32),
            "rel": vmem((PARTS * HALF, width), f32),
            "table": vmem((PARTS, NC, FOUR, FOUR) + column, bf16),
            "partner": vmem((2, NC, rows, width), bf16),
            "own": vmem((ent, width), bf16),
            "own_t": vmem((width, ent), bf16),
            "par_t": vmem((width, ent), bf16),
            "count": vmem((4, ent, LANES), f32),
            "h": vmem((width, lanes), bf16),
            "t": vmem((width, lanes), bf16),
            "w": vmem((width, lanes), f32),
            "head": vmem((width, ent), f32),
            "tail": vmem((width, ent), f32),
            "rg": vmem((width, lanes), bf16),
            "ent": vmem((2, 2, NC, rows, width), bf16),
            "for_core": vmem((FOUR, PARTS * FOUR) + turned, bf16),
            "from_core": vmem((FOUR, PARTS * FOUR) + turned, bf16),
            "product": vmem((PARTS * FOUR,) + turned, f32),
            "total": vmem((FOUR, PARTS * FOUR) + turned, bf16),
            "in_last": vmem((FOUR, PARTS, FOUR - 1) + turned, bf16),
            "two": vmem((FOUR - 1, PARTS) + turned, bf16),
            "in_second": vmem((FOUR - 1, PARTS) + turned, bf16),
            "three": vmem((PARTS,) + column, bf16),
            "in_z": vmem((PARTS, NZ - 1, HALF, width), bf16),
            "ent_core": vmem((2, 2, rows, width), bf16),
            "ent_half": vmem((2, 2, rows, width), bf16),
            "ent_side": vmem((2, rows, width), bf16),
            "send": pltpu.SemaphoreType.DMA((COPIES,)),
            "recv": pltpu.SemaphoreType.DMA((COPIES,)),
        }
        self.partner = Partner.scratch(rows // 2, width)

    def types(self):
        return list(self.shapes.values()) + self.partner + self.partner

    def bind(self, refs):
        for name, ref in zip(self.shapes, refs):
            setattr(self, name, ref)
        rest = refs[len(self.shapes) :]
        self.there, self.back = rest[:8], rest[8:]


def round_kernel(scratch, block_rows, samples, *refs):
    plan_ref, live_ref, ids_in, head_negs, tail_negs, rel_in, own_in = refs[:7]
    rel_sum_ref, ent_sum_ref = refs[7:9]
    v = scratch
    v.bind(refs[9:])
    f32, bf16 = jnp.float32, jnp.bfloat16
    pos, core = here()
    copies = Copies(v.send, v.recv)
    put = copies.put
    sibling = device(pos, 1 - core)
    x_low = lax.rem(pos["x"], 2)
    ent, width = own_in.shape
    half = width // 2
    rows = ent // 4
    lanes = v.w.shape[1]
    peers = all_peers(pos, core)

    signal_all(peers)
    shard = rel_in.shape[0]
    v.rel[...] = jnp.zeros_like(v.rel)
    v.rel[:shard, :] = rel_in[...]
    for part in range(PARTS):
        slot = v.table.at[part, core, pos[SECOND[part]], pos[LAST[part]], pos["z"]]
        slot[...] = v.rel[part * HALF : (part + 1) * HALF, :].astype(bf16)
    v.own[...] = own_in[...].astype(bf16)
    wait_all(peers)

    along_z = []
    for part in range(PARTS):
        mine = v.table.at[part, core, pos[SECOND[part]], pos[LAST[part]], pos["z"]]
        along_z += [
            put(mine, mine, device(moved(pos, "z", step), core)) for step in range(1, NZ)
        ]
    partner = Partner(copies, pos, core, plan_ref[0], v.there)
    first = pl.multiple_of((x_low * NC + core) * rows, rows)
    for side in range(2):
        partner.send(side, "x", v.own[pl.ds(first + side * (rows // 2), rows // 2), :])

    v.ids[...] = jnp.full_like(v.ids, -1)
    v.ids[:, : ids_in.shape[1]] = ids_in[...]
    v.negs[...] = jnp.full_like(v.negs, -1)
    v.negs[0:2, :samples] = head_negs[...]
    v.negs[2:4, :samples] = tail_negs[...]
    v.own_t[...] = v.own[...].astype(f32).T.astype(bf16)
    v.w[...] = jnp.zeros_like(v.w)
    v.head[...] = jnp.zeros_like(v.head)
    v.tail[...] = jnp.zeros_like(v.tail)

    def tiles(body):
        @pl.loop(0, lanes // TILE)
        def _(tile):
            base = pl.multiple_of(tile * TILE, TILE)
            body(base, pl.ds(base, TILE))

    def gather_heads(base, cols):
        v.h[:, cols] = dot(v.own_t[...], one_hot(v.ids[0:1, cols], 0, ent)).astype(bf16)

    def gather_tails(base, cols):
        v.t[:, cols] = dot(v.par_t[...], one_hot(v.ids[2:3, cols], 0, ent)).astype(bf16)

    tiles(gather_heads)
    ones = jnp.ones((v.negs.shape[1], LANES), bf16)
    for row in range(4):
        v.count[row] = dot(one_hot(v.negs[row : row + 1, :], 0, ent), ones)
    partner.turn("x", "y")
    for copy in along_z:
        copy.wait_recv()

    along_second, along_last = [], []

    def spread(part, step):
        where = moved(pos, SECOND[part], -step)
        column = v.table.at[part, core, where[SECOND[part]], pos[LAST[part]]]
        return [
            put(column, column, device(moved(pos, LAST[part], there), core))
            for there in range(1, FOUR)
        ]

    for part in range(PARTS):
        column = v.table.at[part, core, pos[SECOND[part]], pos[LAST[part]]]
        along_second.append(
            [
                put(column, column, device(moved(pos, SECOND[part], step), core))
                for step in range(1, FOUR)
            ]
        )
    along_last.append([spread(part, 0) for part in range(PARTS)])
    partner.turn("y", "z_hi")
    for step in range(1, FOUR):
        for part in range(PARTS):
            along_second[part][step - 1].wait_recv()
        along_last.append([spread(part, step) for part in range(PARTS)])

    def add_columns(which, places):
        blocks, hots = [], []
        for part, second, last in places:
            blocks.append(v.table[part, which, second, last].reshape(COLUMN, width))
            base = chunk_base(part, which, second) + last * COLUMN
            hots.append(one_hot(v.ids[1:2, :], base, COLUMN))
        v.w[...] += dot(jnp.concatenate(blocks, axis=0), jnp.concatenate(hots, axis=0), FIRST)

    def add_early(which):
        add_columns(
            which,
            [
                (part, second, pos[LAST[part]])
                for part in range(PARTS)
                for second in range(FOUR)
            ],
        )

    def others(step):
        return [
            (
                part,
                moved(pos, SECOND[part], -step)[SECOND[part]],
                moved(pos, LAST[part], there)[LAST[part]],
            )
            for part in range(PARTS)
            for there in range(1, FOUR)
        ]

    def add(which, step):
        add_columns(which, others(step))

    early = []
    for part in range(PARTS):
        columns = v.table.at[part, core, :, pos[LAST[part]]]
        early.append(put(columns, columns, sibling))
    across = []

    def cross(step):
        for part in range(PARTS):
            for copy in along_last[step][part]:
                copy.wait_recv()
        columns = [v.table.at[part, core, second, last] for part, second, last in others(step)]
        across.append([put(column, column, sibling) for column in columns])

    def add_across(step):
        for copy in across[step]:
            copy.wait_recv()
        add(1 - core, step)

    add_early(core)
    cross(0)
    add(core, 0)
    for copy in early:
        copy.wait_recv()
    partner.turn("z_hi", "z_lo")
    add_early(1 - core)
    cross(1)
    add_across(0)
    mine = v.partner.at[x_low, core]
    mine[: rows // 2, :] = partner.take(0, "z_lo")
    mine[rows // 2 :, :] = partner.take(1, "z_lo")
    replicas = to_replicas(put, v.partner, pos, core)
    add(core, 1)
    cross(2)
    add_across(1)
    add(core, 2)
    cross(3)
    add_across(2)
    add(core, 3)
    add_across(3)
    for copy in replicas:
        copy.wait_recv()
    v.par_t[...] = v.partner[...].reshape(ent, width).astype(f32).T.astype(bf16)
    tiles(gather_tails)

    def edges(base, cols):
        slot = lax.broadcasted_iota(jnp.int32, (1, TILE), 1) + base
        act = jnp.where(slot < live_ref[0], 1.0, 0.0)
        in_first = slot < block_rows
        par = v.partner[...].reshape(ent, width)
        h, t, w = v.h[:, cols].astype(f32), v.t[:, cols].astype(f32), v.w[:, cols]
        ha, hb, ta, tb, wa, wb = h[:half], h[half:], t[:half], t[half:], w[:half], w[half:]
        query = jnp.concatenate([ha * wa - hb * wb, ha * wb + hb * wa], axis=0)
        probe = jnp.concatenate([wa * ta + wb * tb, wa * tb - wb * ta], axis=0)
        positive = jnp.sum(query * t, axis=0, keepdims=True)
        query_low = query.astype(bf16)
        probe_low = probe.astype(bf16)
        pos_weight = -act * jax.nn.sigmoid(-positive)
        scaling = act / samples

        def weights(scores, row):
            repeats = TILE // LANES
            count = jnp.where(
                in_first,
                jnp.concatenate([v.count[row]] * repeats, axis=1),
                jnp.concatenate([v.count[row + 1]] * repeats, axis=1),
            )
            return (jax.nn.sigmoid(scores) * scaling * count).astype(bf16)

        tail_w = weights(dot(par, query_low), 2)
        head_w = weights(dot(v.own[...], probe_low), 0)
        qg = pos_weight * t + dot(v.par_t[...], tail_w)
        pg = dot(v.own_t[...], head_w)
        qa, qb, pa, pb = qg[:half], qg[half:], pg[:half], pg[half:]
        head_grad = jnp.concatenate([qa * wa + qb * wb, qb * wa - qa * wb], axis=0)
        tail_grad = (
            jnp.concatenate([pa * wa - pb * wb, pa * wb + pb * wa], axis=0) + pos_weight * query
        )
        rel_grad = jnp.concatenate(
            [qa * ha + qb * hb + pa * ta + pb * tb, qb * ha - qa * hb + pa * tb - pb * ta], axis=0
        )
        v.rg[:, cols] = rel_grad.astype(bf16)
        hot_h = one_hot(v.ids[0:1, cols], 0, ent)
        hot_t = one_hot(v.ids[2:3, cols], 0, ent)
        v.head[...] += dot(
            jnp.concatenate([probe_low, head_grad.astype(bf16)], axis=1),
            jnp.concatenate([head_w, hot_h], axis=1),
            INNER,
        )
        v.tail[...] += dot(
            jnp.concatenate([query_low, tail_grad.astype(bf16)], axis=1),
            jnp.concatenate([tail_w, hot_t], axis=1),
            INNER,
        )

    tiles(edges)
    shape = v.ent.shape[1:]
    v.ent[0] = v.head[...].T.astype(bf16).reshape(shape)
    v.ent[1] = v.tail[...].T.astype(bf16).reshape(shape)

    ent_copy = put(v.ent.at[:, :, 1 - core], v.ent_core, sibling)

    def chunk(which, step, out, kind):
        hots = []
        for part in range(PARTS):
            second = moved(pos, SECOND[part], step)[SECOND[part]]
            hots.append(one_hot(v.ids[1:2, :], chunk_base(part, which, second), CHUNK))
        summed = dot(v.rg[...], jnp.concatenate(hots, axis=0), INNER).astype(kind)
        for column in range(PARTS * FOUR):
            out[column] = summed[:, column * COLUMN : (column + 1) * COLUMN]

    def for_sibling(step):
        chunk(1 - core, step, v.for_core.at[step], bf16)
        return put(v.for_core.at[step], v.from_core.at[step], sibling)

    def for_chips(step, core_copy):
        chunk(core, step, v.product, f32)
        core_copy.wait_recv()
        v.total[step] = (v.product[...] + v.from_core[step].astype(f32)).astype(bf16)
        flying = []
        for part in range(PARTS):
            for there in range(1, FOUR):
                target = moved(pos, LAST[part], there)
                flying.append(
                    put(
                        v.total.at[step, part * FOUR + target[LAST[part]]],
                        v.in_last.at[step, part, there - 1],
                        device(target, core),
                    )
                )
        return flying

    def sum_last(step, part):
        value = v.total[step, part * FOUR + pos[LAST[part]]].astype(f32)
        for there in range(FOUR - 1):
            value += v.in_last[step, part, there].astype(f32)
        return value

    def to_second(step, flying):
        for copy in flying:
            copy.wait_recv()
        started = []
        for part in range(PARTS):
            v.two[step - 1, part] = sum_last(step, part).astype(bf16)
            started.append(
                put(
                    v.two.at[step - 1, part],
                    v.in_second.at[step - 1, part],
                    device(moved(pos, SECOND[part], step), core),
                )
            )
        return started

    partner = Partner(copies, pos, core, plan_ref[0], v.back)
    core_copy = for_sibling(1)
    ent_copy.wait_recv()
    v.ent_half[...] = (v.ent[:, :, core].astype(f32) + v.ent_core[...].astype(f32)).astype(bf16)
    side_copy = put(v.ent_half.at[:, 1 - x_low], v.ent_side, device(beside(pos), core))
    flying_1 = for_chips(1, core_copy)
    core_copy = for_sibling(2)
    flying_2 = for_chips(2, core_copy)
    side_copy.wait_recv()
    piece = (v.ent_half[1, x_low].astype(f32) + v.ent_side[1].astype(f32)).astype(bf16)
    partner.send(0, "z_hi", piece[: rows // 2])
    partner.send(1, "z_hi", piece[rows // 2 :])
    core_copy = for_sibling(3)
    seconds = to_second(1, flying_1)
    flying_3 = for_chips(3, core_copy)
    core_copy = for_sibling(0)
    seconds += to_second(2, flying_2)
    flying_0 = for_chips(0, core_copy)
    partner.turn("z_hi", "z_lo")
    seconds += to_second(3, flying_3)
    for copy in flying_0:
        copy.wait_recv()
    own = [sum_last(0, part) for part in range(PARTS)]
    partner.turn("z_lo", "y")
    for copy in seconds:
        copy.wait_recv()
    last_z = []
    for part in range(PARTS):
        value = own[part]
        for step in range(FOUR - 1):
            value += v.in_second[step, part].astype(f32)
        v.three[part] = value.T.astype(bf16).reshape(v.three.shape[1:])
        for step in range(1, NZ):
            target = moved(pos, "z", step)
            last_z.append(
                put(
                    v.three.at[part, target["z"]],
                    v.in_z.at[part, step - 1],
                    device(target, core),
                )
            )
    partner.turn("y", "x")
    mine = ent_sum_ref.at[x_low, core]
    held = v.ent_half[0, x_low].astype(f32) + v.ent_side[0].astype(f32)
    for side in range(2):
        some = slice(side * (rows // 2), (side + 1) * (rows // 2))
        mine[some, :] = (held[some] + partner.take(side, "x").astype(f32)).astype(bf16)
    replicas = to_replicas(put, ent_sum_ref, pos, core)
    for copy in last_z:
        copy.wait_recv()
    for part in range(PARTS):
        value = v.three[part, pos["z"]].astype(f32)
        for step in range(NZ - 1):
            value += v.in_z[part, step].astype(f32)
        rel_sum_ref[part] = value
    for copy in replicas:
        copy.wait_recv()
    copies.finish()


def whole_round(plan, live, ids, head_negs, tail_negs, rel, own, block_rows):
    ent, width = own.shape
    samples = head_negs.shape[1]
    lanes = -(-ids.shape[1] // TILE) * TILE
    scratch = Scratch(ent, width, lanes, samples)
    smem = pl.BlockSpec(memory_space=pltpu.SMEM)
    vmem = pl.BlockSpec(memory_space=pltpu.VMEM)
    return pl.pallas_call(
        functools.partial(round_kernel, scratch, block_rows, samples),
        out_shape=(
            jax.ShapeDtypeStruct((PARTS, HALF, width), jnp.float32),
            jax.ShapeDtypeStruct((2, NC, ent // 4, width), jnp.bfloat16),
        ),
        in_specs=[smem] * 2 + [vmem] * 5,
        out_specs=(vmem,) * 2,
        scratch_shapes=scratch.types(),
        compiler_params=pltpu.CompilerParams(
            collective_id=0, has_side_effects=True, vmem_limit_bytes=VMEM_LIMIT
        ),
    )(plan, live, ids, head_negs, tail_negs, rel, own)


def adagrad(param, state, grad):
    new_state = state + jnp.mean(grad * grad, axis=1)
    return (param - LEARN * grad / jnp.sqrt(new_state)[:, None], new_state)


def table_rows(ids, shard):
    owner, row = ids // shard, ids % shard
    dom, rep = owner // 4, owner % 4
    y, x, z = dom // (2 * NZ), (dom // NZ) % 2 * 2 + rep // 2, dom % NZ
    part = row // HALF
    second, last = at_part(part, y, x), at_part(part, x, y)
    return (((part * NC + rep % 2) * FOUR + second) * FOUR + last) * NZ * HALF + (
        z * HALF + row % HALF
    )


def local(
    entities,
    entity_state,
    relations,
    relation_state,
    head_ids,
    relation_ids,
    tail_ids,
    head_negatives,
    tail_negatives,
    bucket_sizes,
    plan,
):
    ent_rows, width = entities.shape
    shard = relations.shape[0]
    edge_slots = head_ids.shape[0]
    ids = jnp.stack([head_ids, table_rows(relation_ids, shard), tail_ids])
    live = jnp.minimum(bucket_sizes - lax.axis_index("rep") * edge_slots, edge_slots)
    relation_sum, summed = whole_round(
        plan,
        live,
        ids,
        head_negatives,
        tail_negatives,
        relations,
        entities,
        edge_slots // head_negatives.shape[0],
    )
    summed = summed.reshape(ent_rows, width).astype(jnp.float32)
    new_entities, new_entity_state = adagrad(entities, entity_state, summed)
    relation_sum = relation_sum.reshape(PARTS * HALF, width)[:shard]
    new_relations, new_relation_state = adagrad(relations, relation_state, relation_sum)
    return (new_entities, new_entity_state, new_relations, new_relation_state)


def solution(mesh):
    placed = (
        P("dom", None),
        P("dom"),
        P(("dom", "rep"), None),
        P(("dom", "rep")),
        P(("dom", "rep")),
        P(("dom", "rep")),
        P(("dom", "rep")),
        P(("dom", "rep"), None),
        P(("dom", "rep"), None),
        P("dom"),
        P(),
    )
    return jax.shard_map(
        local,
        mesh=mesh,
        in_specs=placed,
        out_specs=(P("dom", None), P("dom"), P(("dom", "rep"), None), P(("dom", "rep"))),
        check_vma=False,
    )
```

```python
import functools

import jax
import jax.numpy as jnp
from jax import lax
from jax.experimental import pallas as pl
from jax.experimental.pallas import tpu as pltpu
from jax.sharding import PartitionSpec as P

LEARN = 0.1
NX, NY, NZ, NC = 4, 4, 8, 2
SIZES = {"x": NX, "y": NY, "z": NZ}
PARTS, HALF = 2, 16
SECOND, LAST = ("y", "x"), ("x", "y")
FOUR = 4
MESH = pl.DeviceIdType.MESH
VMEM_LIMIT = 56 * 1024 * 1024
COLUMN = NZ * HALF
CHUNK = FOUR * COLUMN
TILE = 1024
LANES = 128
INNER = (((1,), (1,)), ((), ()))
FIRST = (((0,), (0,)), ((), ()))


def here():
    dom = lax.axis_index("dom")
    rep = lax.axis_index("rep")
    pos = {
        "y": dom // (2 * NZ),
        "x": lax.rem(dom // NZ, 2) * 2 + rep // 2,
        "z": lax.rem(dom, NZ),
    }
    return pos, lax.rem(rep, 2)


def device(pos, core):
    dom = pos["y"] * (2 * NZ) + (pos["x"] // 2) * NZ + pos["z"]
    rep = lax.rem(pos["x"], 2) * 2 + core
    return (dom, rep)


def moved(pos, axis, offset):
    there = dict(pos)
    there[axis] = lax.rem(pos[axis] + offset + SIZES[axis], SIZES[axis])
    return there


def beside(pos):
    there = dict(pos)
    there["x"] = pos["x"] + 1 - 2 * lax.rem(pos["x"], 2)
    return there


def signal_all(devices):
    barrier = pltpu.get_barrier_semaphore()
    for target in devices:
        pl.semaphore_signal(barrier, inc=1, device_id=target, device_id_type=MESH)


def wait_all(devices):
    pl.semaphore_wait(pltpu.get_barrier_semaphore(), len(devices))


def all_peers(pos, core):
    peers = [device(pos, 1 - core), device(beside(pos), 1 - core)]
    for axis, count in SIZES.items():
        peers += [device(moved(pos, axis, step), core) for step in range(1, count)]
    return peers


COPIES = 176


class Copies:
    def __init__(self, send, recv):
        self.send, self.recv, self.started = send, recv, []

    def put(self, source, target, device_id):
        index = len(self.started)
        assert index < COPIES
        copy = pltpu.make_async_remote_copy(
            src_ref=source,
            dst_ref=target,
            send_sem=self.send.at[index],
            recv_sem=self.recv.at[index],
            device_id=device_id,
            device_id_type=MESH,
        )
        copy.start()
        self.started.append(copy)
        return copy

    def finish(self):
        for copy in self.started:
            copy.wait_send()


class Partner:
    COUNTS = {"x": 2, "y": NY, "z_hi": NZ // 2, "z_lo": 2}

    def __init__(self, copies, pos, core, mask, refs):
        self.copies, self.pos, self.core = copies, pos, core
        names = list(self.COUNTS)
        self.buffers = [dict(zip(names, refs[:4])), dict(zip(names, refs[4:8]))]
        self.index = {
            "x": pos["x"] // 2,
            "y": pos["y"],
            "z_hi": pos["z"] // 2,
            "z_lo": lax.rem(pos["z"], 2),
        }
        self.bits = {
            "x": mask // NZ % 2,
            "y": mask // (2 * NZ),
            "z_hi": mask % NZ // 2,
            "z_lo": mask % 2,
        }
        self.flying = {}

    def peers(self, axis):
        pos = self.pos
        if axis == "x":
            return [moved(pos, "x", 2)]
        if axis == "y":
            return [moved(pos, "y", step) for step in range(1, NY)]
        if axis == "z_hi":
            return [moved(pos, "z", step) for step in range(2, NZ, 2)]
        return [moved(pos, "z", 1 - 2 * self.index["z_lo"])]

    def send(self, half, axis, rows):
        mine = self.buffers[half][axis].at[self.index[axis]]
        mine[...] = rows
        self.flying[half, axis] = [
            self.copies.put(mine, mine, device(there, self.core)) for there in self.peers(axis)
        ]

    def take(self, half, axis):
        for copy in self.flying[half, axis]:
            copy.wait_recv()
        return self.buffers[half][axis][jnp.bitwise_xor(self.index[axis], self.bits[axis])]

    def turn(self, axis, following):
        for half in range(2):
            self.send(half, following, self.take(half, axis))

    @classmethod
    def scratch(cls, rows, width):
        return [
            pltpu.VMEM((count, rows, width), jnp.bfloat16)
            for _ in range(2)
            for count in cls.COUNTS.values()
        ]


def to_replicas(put, whole, pos, core, some):
    mine = whole.at[lax.rem(pos["x"], 2), core, some]
    others = [device(beside(pos), core), device(beside(pos), 1 - core), device(pos, 1 - core)]
    return [put(mine, mine, target) for target in others]


def dot(a, b, dims=(((1,), (0,)), ((), ()))):
    return lax.dot_general(a, b, dims, preferred_element_type=jnp.float32)


def one_hot(ids, base, count):
    rows = lax.broadcasted_iota(jnp.int32, (count, ids.shape[1]), 0)
    return jnp.where(rows == ids - base, 1.0, 0.0).astype(jnp.bfloat16)


def at_part(part, first, second):
    return first + part * (second - first)


def chunk_base(part, core, second):
    return ((part * NC + core) * FOUR + second) * CHUNK


class Scratch:
    def __init__(self, ent, width, lanes, samples):
        rows = ent // 4
        bf16, f32 = jnp.bfloat16, jnp.float32
        column = (NZ, HALF, width)
        turned = (width, COLUMN)
        vmem = pltpu.VMEM
        self.shapes = {
            "ids": vmem((3, lanes), jnp.int32),
            "negs": vmem((4, -(-samples // LANES) * LANES), jnp.int32),
            "rel": vmem((PARTS * HALF, width), f32),
            "table": vmem((PARTS, NC, FOUR, FOUR) + column, bf16),
            "partner": vmem((2, NC, rows, width), bf16),
            "own": vmem((ent, width), bf16),
            "own_t": vmem((width, ent), bf16),
            "par_t": vmem((width, ent), bf16),
            "count": vmem((4, ent, LANES), f32),
            "h": vmem((width, lanes), bf16),
            "t": vmem((width, lanes), bf16),
            "w": vmem((width, lanes), f32),
            "head": vmem((width, ent), f32),
            "tail": vmem((width, ent), f32),
            "rg": vmem((width, lanes), bf16),
            "ent": vmem((2, 2, NC, rows, width), bf16),
            "for_core": vmem((FOUR, PARTS * FOUR) + turned, bf16),
            "from_core": vmem((FOUR, PARTS * FOUR) + turned, bf16),
            "product": vmem((PARTS * FOUR,) + turned, f32),
            "total": vmem((FOUR, PARTS * FOUR) + turned, bf16),
            "in_last": vmem((FOUR, PARTS, FOUR - 1) + turned, bf16),
            "two": vmem((FOUR - 1, PARTS) + turned, bf16),
            "in_second": vmem((FOUR - 1, PARTS) + turned, bf16),
            "three": vmem((PARTS,) + column, bf16),
            "in_z": vmem((PARTS, NZ - 1, HALF, width), bf16),
            "ent_core": vmem((2, 2, rows, width), bf16),
            "ent_half": vmem((2, 2, rows, width), bf16),
            "ent_side": vmem((2, rows, width), bf16),
            "send": pltpu.SemaphoreType.DMA((COPIES,)),
            "recv": pltpu.SemaphoreType.DMA((COPIES,)),
        }
        self.partner = Partner.scratch(rows // 2, width)

    def types(self):
        return list(self.shapes.values()) + self.partner + self.partner

    def bind(self, refs):
        for name, ref in zip(self.shapes, refs):
            setattr(self, name, ref)
        rest = refs[len(self.shapes) :]
        self.there, self.back = rest[:8], rest[8:]


def round_kernel(scratch, block_rows, samples, *refs):
    plan_ref, live_ref, ids_in, head_negs, tail_negs, rel_in, own_in = refs[:7]
    rel_sum_ref, ent_sum_ref = refs[7:9]
    v = scratch
    v.bind(refs[9:])
    f32, bf16 = jnp.float32, jnp.bfloat16
    pos, core = here()
    copies = Copies(v.send, v.recv)
    put = copies.put
    sibling = device(pos, 1 - core)
    x_low = lax.rem(pos["x"], 2)
    ent, width = own_in.shape
    half = width // 2
    rows = ent // 4
    lanes = v.w.shape[1]
    peers = all_peers(pos, core)

    signal_all(peers)
    shard = rel_in.shape[0]
    v.rel[...] = jnp.zeros_like(v.rel)
    v.rel[:shard, :] = rel_in[...]
    for part in range(PARTS):
        slot = v.table.at[part, core, pos[SECOND[part]], pos[LAST[part]], pos["z"]]
        slot[...] = v.rel[part * HALF : (part + 1) * HALF, :].astype(bf16)
    v.own[...] = own_in[...].astype(bf16)
    wait_all(peers)

    along_z = []
    for part in range(PARTS):
        mine = v.table.at[part, core, pos[SECOND[part]], pos[LAST[part]], pos["z"]]
        along_z += [
            put(mine, mine, device(moved(pos, "z", step), core)) for step in range(1, NZ)
        ]
    partner = Partner(copies, pos, core, plan_ref[0], v.there)
    first = pl.multiple_of((x_low * NC + core) * rows, rows)
    for side in range(2):
        partner.send(side, "x", v.own[pl.ds(first + side * (rows // 2), rows // 2), :])

    v.ids[...] = jnp.full_like(v.ids, -1)
    v.ids[:, : ids_in.shape[1]] = ids_in[...]
    v.negs[...] = jnp.full_like(v.negs, -1)
    v.negs[0:2, :samples] = head_negs[...]
    v.negs[2:4, :samples] = tail_negs[...]
    v.own_t[...] = v.own[...].astype(f32).T.astype(bf16)
    v.w[...] = jnp.zeros_like(v.w)
    v.head[...] = jnp.zeros_like(v.head)
    v.tail[...] = jnp.zeros_like(v.tail)

    def tiles(body):
        @pl.loop(0, lanes // TILE)
        def _(tile):
            base = pl.multiple_of(tile * TILE, TILE)
            body(base, pl.ds(base, TILE))

    def gather_heads(base, cols):
        v.h[:, cols] = dot(v.own_t[...], one_hot(v.ids[0:1, cols], 0, ent)).astype(bf16)

    def gather_tails(base, cols):
        v.t[:, cols] = dot(v.par_t[...], one_hot(v.ids[2:3, cols], 0, ent)).astype(bf16)

    tiles(gather_heads)
    ones = jnp.ones((v.negs.shape[1], LANES), bf16)
    for row in range(4):
        v.count[row] = dot(one_hot(v.negs[row : row + 1, :], 0, ent), ones)
    partner.turn("x", "y")
    for copy in along_z:
        copy.wait_recv()

    along_second, along_last = [], []

    def spread(part, step):
        where = moved(pos, SECOND[part], -step)
        column = v.table.at[part, core, where[SECOND[part]], pos[LAST[part]]]
        return [
            put(column, column, device(moved(pos, LAST[part], there), core))
            for there in range(1, FOUR)
        ]

    for part in range(PARTS):
        column = v.table.at[part, core, pos[SECOND[part]], pos[LAST[part]]]
        along_second.append(
            [
                put(column, column, device(moved(pos, SECOND[part], step), core))
                for step in range(1, FOUR)
            ]
        )
    along_last.append([spread(part, 0) for part in range(PARTS)])
    partner.turn("y", "z_hi")
    for step in range(1, FOUR):
        for part in range(PARTS):
            along_second[part][step - 1].wait_recv()
        along_last.append([spread(part, step) for part in range(PARTS)])

    def add_columns(which, places):
        blocks, hots = [], []
        for part, second, last in places:
            blocks.append(v.table[part, which, second, last].reshape(COLUMN, width))
            base = chunk_base(part, which, second) + last * COLUMN
            hots.append(one_hot(v.ids[1:2, :], base, COLUMN))
        v.w[...] += dot(jnp.concatenate(blocks, axis=0), jnp.concatenate(hots, axis=0), FIRST)

    def add_early(which):
        add_columns(
            which,
            [
                (part, second, pos[LAST[part]])
                for part in range(PARTS)
                for second in range(FOUR)
            ],
        )

    def others(step):
        return [
            (
                part,
                moved(pos, SECOND[part], -step)[SECOND[part]],
                moved(pos, LAST[part], there)[LAST[part]],
            )
            for part in range(PARTS)
            for there in range(1, FOUR)
        ]

    def add(which, step):
        add_columns(which, others(step))

    early = []
    for part in range(PARTS):
        columns = v.table.at[part, core, :, pos[LAST[part]]]
        early.append(put(columns, columns, sibling))
    across = []

    def cross(step):
        for part in range(PARTS):
            for copy in along_last[step][part]:
                copy.wait_recv()
        columns = [v.table.at[part, core, second, last] for part, second, last in others(step)]
        across.append([put(column, column, sibling) for column in columns])

    def add_across(step):
        for copy in across[step]:
            copy.wait_recv()
        add(1 - core, step)

    add_early(core)
    cross(0)
    add(core, 0)
    for copy in early:
        copy.wait_recv()
    partner.turn("z_hi", "z_lo")
    add_early(1 - core)
    cross(1)
    add_across(0)
    replicas = []
    for side in range(2):
        some = pl.ds(side * (rows // 2), rows // 2)
        v.partner[x_low, core, some, :] = partner.take(side, "z_lo")
        replicas += to_replicas(put, v.partner, pos, core, some)
    add(core, 1)
    cross(2)
    add_across(1)
    add(core, 2)
    cross(3)
    add_across(2)
    add(core, 3)
    add_across(3)
    for copy in replicas:
        copy.wait_recv()
    v.par_t[...] = v.partner[...].reshape(ent, width).astype(f32).T.astype(bf16)
    tiles(gather_tails)

    def edges(base, cols):
        slot = lax.broadcasted_iota(jnp.int32, (1, TILE), 1) + base
        act = jnp.where(slot < live_ref[0], 1.0, 0.0)
        in_first = slot < block_rows
        par = v.partner[...].reshape(ent, width)
        h, t, w = v.h[:, cols].astype(f32), v.t[:, cols].astype(f32), v.w[:, cols]
        ha, hb, ta, tb, wa, wb = h[:half], h[half:], t[:half], t[half:], w[:half], w[half:]
        query = jnp.concatenate([ha * wa - hb * wb, ha * wb + hb * wa], axis=0)
        probe = jnp.concatenate([wa * ta + wb * tb, wa * tb - wb * ta], axis=0)
        positive = jnp.sum(query * t, axis=0, keepdims=True)
        query_low = query.astype(bf16)
        probe_low = probe.astype(bf16)
        pos_weight = -act * jax.nn.sigmoid(-positive)
        scaling = act / samples

        def weights(scores, row):
            repeats = TILE // LANES
            count = jnp.where(
                in_first,
                jnp.concatenate([v.count[row]] * repeats, axis=1),
                jnp.concatenate([v.count[row + 1]] * repeats, axis=1),
            )
            return (jax.nn.sigmoid(scores) * scaling * count).astype(bf16)

        tail_w = weights(dot(par, query_low), 2)
        head_w = weights(dot(v.own[...], probe_low), 0)
        qg = pos_weight * t + dot(v.par_t[...], tail_w)
        pg = dot(v.own_t[...], head_w)
        qa, qb, pa, pb = qg[:half], qg[half:], pg[:half], pg[half:]
        head_grad = jnp.concatenate([qa * wa + qb * wb, qb * wa - qa * wb], axis=0)
        tail_grad = (
            jnp.concatenate([pa * wa - pb * wb, pa * wb + pb * wa], axis=0) + pos_weight * query
        )
        rel_grad = jnp.concatenate(
            [qa * ha + qb * hb + pa * ta + pb * tb, qb * ha - qa * hb + pa * tb - pb * ta], axis=0
        )
        v.rg[:, cols] = rel_grad.astype(bf16)
        hot_h = one_hot(v.ids[0:1, cols], 0, ent)
        hot_t = one_hot(v.ids[2:3, cols], 0, ent)
        v.head[...] += dot(
            jnp.concatenate([probe_low, head_grad.astype(bf16)], axis=1),
            jnp.concatenate([head_w, hot_h], axis=1),
            INNER,
        )
        v.tail[...] += dot(
            jnp.concatenate([query_low, tail_grad.astype(bf16)], axis=1),
            jnp.concatenate([tail_w, hot_t], axis=1),
            INNER,
        )

    tiles(edges)
    shape = v.ent.shape[1:]
    v.ent[0] = v.head[...].T.astype(bf16).reshape(shape)
    v.ent[1] = v.tail[...].T.astype(bf16).reshape(shape)

    ent_copies = {
        side: put(v.ent.at[side, :, 1 - core], v.ent_core.at[side], sibling) for side in (1, 0)
    }

    def chunk(which, step, out, kind):
        hots = []
        for part in range(PARTS):
            second = moved(pos, SECOND[part], step)[SECOND[part]]
            hots.append(one_hot(v.ids[1:2, :], chunk_base(part, which, second), CHUNK))
        summed = dot(v.rg[...], jnp.concatenate(hots, axis=0), INNER).astype(kind)
        for column in range(PARTS * FOUR):
            out[column] = summed[:, column * COLUMN : (column + 1) * COLUMN]

    def for_sibling(step):
        chunk(1 - core, step, v.for_core.at[step], bf16)
        return put(v.for_core.at[step], v.from_core.at[step], sibling)

    def for_chips(step, core_copy):
        chunk(core, step, v.product, f32)
        core_copy.wait_recv()
        v.total[step] = (v.product[...] + v.from_core[step].astype(f32)).astype(bf16)
        flying = []
        for part in range(PARTS):
            for there in range(1, FOUR):
                target = moved(pos, LAST[part], there)
                flying.append(
                    put(
                        v.total.at[step, part * FOUR + target[LAST[part]]],
                        v.in_last.at[step, part, there - 1],
                        device(target, core),
                    )
                )
        return flying

    def sum_last(step, part):
        value = v.total[step, part * FOUR + pos[LAST[part]]].astype(f32)
        for there in range(FOUR - 1):
            value += v.in_last[step, part, there].astype(f32)
        return value

    def to_second(step, flying):
        for copy in flying:
            copy.wait_recv()
        started = []
        for part in range(PARTS):
            v.two[step - 1, part] = sum_last(step, part).astype(bf16)
            started.append(
                put(
                    v.two.at[step - 1, part],
                    v.in_second.at[step - 1, part],
                    device(moved(pos, SECOND[part], step), core),
                )
            )
        return started

    partner = Partner(copies, pos, core, plan_ref[0], v.back)
    core_copy = for_sibling(1)
    side_copies = {}
    for side in (1, 0):
        ent_copies[side].wait_recv()
        v.ent_half[side] = (
            v.ent[side, :, core].astype(f32) + v.ent_core[side].astype(f32)
        ).astype(bf16)
        side_copies[side] = put(
            v.ent_half.at[side, 1 - x_low], v.ent_side.at[side], device(beside(pos), core)
        )
    flying_1 = for_chips(1, core_copy)
    core_copy = for_sibling(2)
    side_copies[1].wait_recv()
    piece = (v.ent_half[1, x_low].astype(f32) + v.ent_side[1].astype(f32)).astype(bf16)
    partner.send(0, "z_hi", piece[: rows // 2])
    partner.send(1, "z_hi", piece[rows // 2 :])
    flying_2 = for_chips(2, core_copy)
    core_copy = for_sibling(3)
    seconds = to_second(1, flying_1)
    flying_3 = for_chips(3, core_copy)
    core_copy = for_sibling(0)
    seconds += to_second(2, flying_2)
    flying_0 = for_chips(0, core_copy)
    partner.turn("z_hi", "z_lo")
    seconds += to_second(3, flying_3)
    for copy in flying_0:
        copy.wait_recv()
    own = [sum_last(0, part) for part in range(PARTS)]
    partner.turn("z_lo", "y")
    for copy in seconds:
        copy.wait_recv()
    last_z = []
    for part in range(PARTS):
        value = own[part]
        for step in range(FOUR - 1):
            value += v.in_second[step, part].astype(f32)
        v.three[part] = value.T.astype(bf16).reshape(v.three.shape[1:])
        for step in range(1, NZ):
            target = moved(pos, "z", step)
            last_z.append(
                put(
                    v.three.at[part, target["z"]],
                    v.in_z.at[part, step - 1],
                    device(target, core),
                )
            )
    partner.turn("y", "x")
    side_copies[0].wait_recv()
    held = v.ent_half[0, x_low].astype(f32) + v.ent_side[0].astype(f32)
    replicas = []
    for side in range(2):
        some = pl.ds(side * (rows // 2), rows // 2)
        ours = held[side * (rows // 2) : (side + 1) * (rows // 2)]
        ent_sum_ref[x_low, core, some, :] = (
            ours + partner.take(side, "x").astype(f32)
        ).astype(bf16)
        replicas += to_replicas(put, ent_sum_ref, pos, core, some)
    for copy in last_z:
        copy.wait_recv()
    for part in range(PARTS):
        value = v.three[part, pos["z"]].astype(f32)
        for step in range(NZ - 1):
            value += v.in_z[part, step].astype(f32)
        rel_sum_ref[part] = value
    for copy in replicas:
        copy.wait_recv()
    copies.finish()


def whole_round(plan, live, ids, head_negs, tail_negs, rel, own, block_rows):
    ent, width = own.shape
    samples = head_negs.shape[1]
    lanes = -(-ids.shape[1] // TILE) * TILE
    scratch = Scratch(ent, width, lanes, samples)
    smem = pl.BlockSpec(memory_space=pltpu.SMEM)
    vmem = pl.BlockSpec(memory_space=pltpu.VMEM)
    return pl.pallas_call(
        functools.partial(round_kernel, scratch, block_rows, samples),
        out_shape=(
            jax.ShapeDtypeStruct((PARTS, HALF, width), jnp.float32),
            jax.ShapeDtypeStruct((2, NC, ent // 4, width), jnp.bfloat16),
        ),
        in_specs=[smem] * 2 + [vmem] * 5,
        out_specs=(vmem,) * 2,
        scratch_shapes=scratch.types(),
        compiler_params=pltpu.CompilerParams(
            collective_id=0, has_side_effects=True, vmem_limit_bytes=VMEM_LIMIT
        ),
    )(plan, live, ids, head_negs, tail_negs, rel, own)


def adagrad(param, state, grad):
    new_state = state + jnp.mean(grad * grad, axis=1)
    return (param - LEARN * grad / jnp.sqrt(new_state)[:, None], new_state)


def table_rows(ids, shard):
    owner, row = ids // shard, ids % shard
    dom, rep = owner // 4, owner % 4
    y, x, z = dom // (2 * NZ), (dom // NZ) % 2 * 2 + rep // 2, dom % NZ
    part = row // HALF
    second, last = at_part(part, y, x), at_part(part, x, y)
    return (((part * NC + rep % 2) * FOUR + second) * FOUR + last) * NZ * HALF + (
        z * HALF + row % HALF
    )


def local(
    entities,
    entity_state,
    relations,
    relation_state,
    head_ids,
    relation_ids,
    tail_ids,
    head_negatives,
    tail_negatives,
    bucket_sizes,
    plan,
):
    ent_rows, width = entities.shape
    shard = relations.shape[0]
    edge_slots = head_ids.shape[0]
    ids = jnp.stack([head_ids, table_rows(relation_ids, shard), tail_ids])
    live = jnp.minimum(bucket_sizes - lax.axis_index("rep") * edge_slots, edge_slots)
    relation_sum, summed = whole_round(
        plan,
        live,
        ids,
        head_negatives,
        tail_negatives,
        relations,
        entities,
        edge_slots // head_negatives.shape[0],
    )
    summed = summed.reshape(ent_rows, width).astype(jnp.float32)
    new_entities, new_entity_state = adagrad(entities, entity_state, summed)
    relation_sum = relation_sum.reshape(PARTS * HALF, width)[:shard]
    new_relations, new_relation_state = adagrad(relations, relation_state, relation_sum)
    return (new_entities, new_entity_state, new_relations, new_relation_state)


def solution(mesh):
    placed = (
        P("dom", None),
        P("dom"),
        P(("dom", "rep"), None),
        P(("dom", "rep")),
        P(("dom", "rep")),
        P(("dom", "rep")),
        P(("dom", "rep")),
        P(("dom", "rep"), None),
        P(("dom", "rep"), None),
        P("dom"),
        P(),
    )
    return jax.shard_map(
        local,
        mesh=mesh,
        in_specs=placed,
        out_specs=(P("dom", None), P("dom"), P(("dom", "rep"), None), P(("dom", "rep"))),
        check_vma=False,
    )
```
